32 devices in a mesh: cols: 32 (over z, y, x, core).
Axes of the slice: x: 2, y: 2, z: 4, core: 2. Of those that a mesh axis runs over, the one named last changes fastest.
Arguments:
- voxel_rows: bfloat16 [768, 32768], P(None, 'cols'), may hold values from -6 to 6
- factor_weight: bfloat16 [5, 2, 32768, 128], P(None, None, 'cols'), may hold values from -0.375 to 0.375
- extra_weight: bfloat16 [32, 128, 128], P('cols'), may hold values from -0.5 to 0.5
- extra_pairs: int32 [32, 2], replicated, may hold values from 0 to 255, as said below
- tile_owner: int32 [32], replicated, may hold values from 0 to 31, each once
Outputs:
- latent: bfloat16 [768, 32768], P(None, 'cols')
The draws below stay inside these ranges and needn't reach their ends.
Inputs may be any that keep to these rules, and one draw needn't show every extreme that they name: `extra_pairs`: extra block k takes its column block from device k's blocks, k * 8 to (k + 1) * 8 - 1; its row block lies on a device whose index differs from k in exactly one bit. `tile_owner`: each device stores the matrix of exactly one extra block.
All inputs are finite; a program needn't handle non-finite values.
Results may differ from the reference program's by a relative error of at most 0.014.
Values may be sent and summed in bfloat16 or wider, within the bound.
A program may use at most 64 MiB of HBM per device.

```python
import jax
import jax.numpy as jnp
from jax import lax

BLOCK = 128
BLK_DEV = 8
BATCH = 768
NBLK = 256
WIDTH = 32768
SECTIONS = 5
NEXTRA = 32


def draw_extra_pairs(key, part):
    index = jnp.arange(NEXTRA, dtype=jnp.int32)
    key_col = jax.random.fold_in(key, 11)
    key_bit = jax.random.fold_in(key, 23)
    key_row = jax.random.fold_in(key, 37)
    col_offset = jax.random.randint(key_col, (NEXTRA,), 0, BLK_DEV, dtype=jnp.int32)
    col_offset = jnp.where(index == 0, 0, jnp.where(index == NEXTRA - 1, BLK_DEV - 1, col_offset))
    bit_choice = jax.random.randint(key_bit, (NEXTRA,), 0, SECTIONS, dtype=jnp.int32)
    bit_choice = jnp.where((index == 1) | (index == NEXTRA - 2), 0, bit_choice)
    row_device = jnp.bitwise_xor(index, jnp.left_shift(jnp.int32(1), bit_choice))
    row_offset = jax.random.randint(key_row, (NEXTRA,), 0, BLK_DEV, dtype=jnp.int32)
    row_offset = jnp.where(index == 1, 0, jnp.where(index == NEXTRA - 2, BLK_DEV - 1, row_offset))
    row_block = row_device * BLK_DEV + row_offset
    col_block = index * BLK_DEV + col_offset
    return jnp.stack([row_block, col_block], axis=1).astype(jnp.int32)


def shard_levels(rng, shape, split, smallest, top_value):
    level, own = 1.0, jax.random.fold_in(rng, 6)
    for position, parts in split:
        steps = jnp.exp(jax.random.uniform(jax.random.fold_in(own, position), (parts,), jnp.float32, smallest / len(split), top_value / len(split)))
        level = level * jnp.repeat(steps, shape[position] // parts).reshape([-1 if axis == position else 1 for axis in range(len(shape))])
    return level


def scatter_about(own_key, shape, width, limit, pieces=(), kind=jnp.bfloat16):
    level = shard_levels(own_key, shape, pieces, -0.22, 0.18) if pieces else 1.0
    array = jax.random.normal(own_key, shape, jnp.float32) * width * level
    return jnp.minimum(jnp.maximum(array, -limit), limit).astype(kind)


def setup_inputs(seed: int = 0) -> dict:
    key_of = jax.random.split(jax.random.key(seed), 6)
    voxel_rows = scatter_about(key_of[0], (BATCH, WIDTH), 1.0, 6.0, ((1, 32),))
    factor_weight = scatter_about(key_of[1], (SECTIONS, 2, WIDTH, BLOCK), (2 * BLOCK) ** -0.5, 0.375, ((2, 32),))
    extra_weight = scatter_about(key_of[2], (NEXTRA, BLOCK, BLOCK), BLOCK ** -0.5, 0.5, ((0, 32),))
    extra_pairs = draw_extra_pairs(jax.random.fold_in(key_of[5], 71), 0)
    tile_owner = jax.random.permutation(key_of[4], NEXTRA).astype(jnp.int32)
    return {"voxel_rows": voxel_rows, "factor_weight": factor_weight, "extra_weight": extra_weight, "extra_pairs": extra_pairs, "tile_owner": tile_owner}


def mix_section(current, weights, distance):
    row_count = current.shape[0]
    groups = NBLK // (2 * distance)
    blocks = current.reshape(row_count, groups, 2, distance, BLOCK).astype(jnp.float32)
    opposite = jnp.flip(blocks, axis=2)
    w_self = weights[0].reshape(groups, 2, distance, BLOCK, BLOCK).astype(jnp.float32)
    w_other = weights[1].reshape(groups, 2, distance, BLOCK, BLOCK).astype(jnp.float32)
    result = jnp.einsum("bgtia,gtiac->bgtic", blocks, w_self)
    result = result + jnp.einsum("bgtia,gtiac->bgtic", opposite, w_other)
    return result.reshape(row_count, WIDTH).astype(jnp.bfloat16)


def reference(voxel_rows, factor_weight, extra_weight, extra_pairs, tile_owner):
    group_size = 128 if BATCH % 128 == 0 else BATCH
    group_count = BATCH // group_size
    tile_table = jnp.take(extra_weight, tile_owner, axis=0).astype(jnp.float32)

    def one_group(group_rows):
        current = group_rows
        for section_number in range(SECTIONS):
            current = mix_section(current, factor_weight[section_number], BLK_DEV * 2 ** section_number)
        inputs = group_rows.reshape(group_size, NBLK, BLOCK)
        picked = jnp.take(inputs, extra_pairs[:, 1], axis=1).astype(jnp.float32)
        contrib = jnp.einsum("bka,kac->bkc", picked, tile_table)
        extra_sum = jnp.zeros((group_size, NBLK, BLOCK), jnp.float32).at[:, extra_pairs[:, 0]].add(contrib)
        total = current.astype(jnp.float32) + extra_sum.reshape(group_size, WIDTH)
        return total.astype(jnp.bfloat16)

    grouped = voxel_rows.reshape(group_count, group_size, WIDTH)
    return lax.map(one_group, grouped).reshape(BATCH, WIDTH)
```

```python
import functools

import jax
import jax.numpy as jnp
from jax import lax
from jax.experimental import pallas as pl
from jax.experimental.pallas import tpu as pltpu
from jax.sharding import PartitionSpec as P

MESH = pl.DeviceIdType.MESH
ROW_PARTS = 2
VMEM_LIMIT = 58 * 1024 * 1024


def butterfly_kernel(
    sections, blocks, parts,
    vox_hbm, factor_hbm, tile_hbm, pairs, owner, out_hbm,
    vox, weights, recv, hidden, result, picked, far_picked, tiles, terms,
    vox_sem, weight_sem, tile_sem, out_sem,
    send_sem, recv_sem, pick_send, pick_recv, tile_send, tile_recv,
):
    me = lax.axis_index("cols")
    chunks, rows, width = vox.shape
    bits = [lax.rem(me // 2**b, 2) for b in range(sections)]
    partners = [me + (1 - 2 * bits[b]) * 2**b for b in range(sections)]
    last = sections - 1
    lag = list(range(last)) + [sections + 2]

    def reverse(number):
        return sum(lax.rem(number // 2**b, 2) * 2 ** (last - b) for b in range(sections))

    my_place = reverse(me)

    def window(ref, c):
        row = pl.multiple_of(lax.rem(c, parts) * rows, rows)
        col = pl.multiple_of((c // parts) * width, width)
        return ref.at[pl.ds(row, rows), pl.ds(col, width)]

    def load_vox(c):
        return pltpu.make_async_copy(window(vox_hbm, c), vox.at[c], vox_sem.at[c])

    def load_weight(s):
        return pltpu.make_async_copy(factor_hbm.at[s], weights.at[s], weight_sem.at[s])

    def store_out(c):
        return pltpu.make_async_copy(result.at[c], window(out_hbm, c), out_sem.at[c])

    def send_section(s, c):
        source = vox.at[c] if s == 0 else hidden.at[s - 1, c]
        return pltpu.make_async_remote_copy(
            src_ref=source, dst_ref=recv.at[s, c],
            send_sem=send_sem.at[s, c], recv_sem=recv_sem.at[s, c],
            device_id=(partners[s],), device_id_type=MESH,
        )

    def send_picked(b):
        return pltpu.make_async_remote_copy(
            src_ref=picked, dst_ref=far_picked.at[b],
            send_sem=pick_send.at[b], recv_sem=pick_recv.at[b],
            device_id=(partners[b],), device_id_type=MESH,
        )

    def send_tiles(g):
        start = (my_place // 2**g) * 2**g
        group = tiles.at[pl.ds(start, 2**g)]
        return pltpu.make_async_remote_copy(
            src_ref=group, dst_ref=group,
            send_sem=tile_send.at[g], recv_sem=tile_recv.at[g],
            device_id=(partners[last - g],), device_id_type=MESH,
        )

    def wait_tiles(g):
        start = (my_place // 2**g) * 2**g
        other = start + (1 - 2 * lax.rem(my_place // 2**g, 2)) * 2**g
        group = tiles.at[pl.ds(other, 2**g)]
        pltpu.make_async_remote_copy(
            src_ref=group, dst_ref=group,
            send_sem=tile_send.at[g], recv_sem=tile_recv.at[g],
            device_id=(partners[last - g],), device_id_type=MESH,
        ).wait_recv()

    tile_load = pltpu.make_async_copy(tile_hbm, tiles.at[pl.ds(my_place, 1)], tile_sem)
    for c in range(chunks):
        load_vox(c).start()
    tile_load.start()
    for s in range(sections):
        load_weight(s).start()

    barrier = pltpu.get_barrier_semaphore()
    for b in range(sections):
        pl.semaphore_signal(barrier, inc=1, device_id=(partners[b],), device_id_type=MESH)
    pl.semaphore_wait(barrier, sections)

    for c in range(chunks):
        load_vox(c).wait()
        send_section(0, c).start()
    offset = jnp.clip(pairs[me, 1] - me * blocks, 0, blocks - 1)
    for part in range(parts):
        picked[part] = vox[offset * parts + part]
    tile_load.wait()
    send_tiles(0).start()
    send_picked(last).start()
    send_picked(last - 1).start()

    pick_step = {b: 2 + b for b in range(last - 1)}
    tile_step = {g: g if g < last - 1 else g + 1 for g in range(1, sections)}

    def compute(s, c):
        i = c // parts
        if s == 0:
            own = vox[c]
        else:
            own = hidden[s - 1, c]
        both = jnp.concatenate([own, recv[s, c]], axis=1)
        place = pl.ds(pl.multiple_of(i * width, width), width)
        factors = jnp.concatenate([weights[s, 0, place, :], weights[s, 1, place, :]], axis=0)
        return jnp.dot(both, factors, preferred_element_type=jnp.float32)

    def step(t, carry):
        for s in range(sections):
            c = t - lag[s]

            @pl.when(c == 0)
            def _():
                load_weight(s).wait()

            if s == last:

                @pl.when(c == 0)
                def _():
                    wait_tiles(last)
                    for b in range(sections):
                        send_picked(b).wait_recv()
                        tile = tiles[reverse(owner[partners[b]])]
                        for part in range(parts):
                            terms[b, part] = jnp.dot(
                                far_picked[b, part], tile, preferred_element_type=jnp.float32
                            )

            @pl.when((c >= 0) & (c < chunks))
            def _():
                send_section(s, c).wait_recv()
                total = compute(s, c)
                if s < last:
                    hidden[s, c] = total.astype(jnp.bfloat16)
                    send_section(s + 1, c).start()
                else:
                    for b in range(sections):
                        slot = pairs[partners[b], 0] - me * blocks
                        mask = jnp.where(slot == c // parts, jnp.float32(1), jnp.float32(0))
                        total = total + mask * terms[b, lax.rem(c, parts)]
                    result[c] = total.astype(jnp.bfloat16)
                    store_out(c).start()

        for b, when in pick_step.items():

            @pl.when(t == when)
            def _():
                send_picked(b).start()

        for g, when in tile_step.items():

            @pl.when(t == when)
            def _():
                wait_tiles(g - 1)
                send_tiles(g).start()

        return carry

    lax.fori_loop(0, chunks + lag[last], step, 0)

    for b in range(sections):
        send_picked(b).wait_send()
        send_tiles(b).wait_send()

    def finish(c, carry):
        for s in range(sections):
            send_section(s, c).wait_send()
        store_out(c).wait()
        return carry

    lax.fori_loop(0, chunks, finish, 0)


def per_device(voxel_rows, factor_weight, extra_weight, extra_pairs, tile_owner):
    devices = lax.axis_size("cols")
    sections = devices.bit_length() - 1
    batch, columns = voxel_rows.shape
    width = extra_weight.shape[1]
    blocks = columns // width
    parts = ROW_PARTS
    rows = batch // parts
    chunks = blocks * parts
    half = jnp.bfloat16
    dma = pltpu.SemaphoreType.DMA
    anywhere = pl.BlockSpec(memory_space=pl.ANY)
    scalars = pl.BlockSpec(memory_space=pltpu.SMEM)
    return pl.pallas_call(
        functools.partial(butterfly_kernel, sections, blocks, parts),
        out_shape=jax.ShapeDtypeStruct(voxel_rows.shape, half),
        in_specs=[anywhere, anywhere, anywhere, scalars, scalars],
        out_specs=anywhere,
        scratch_shapes=[
            pltpu.VMEM((chunks, rows, width), half),
            pltpu.VMEM(factor_weight.shape, half),
            pltpu.VMEM((sections, chunks, rows, width), half),
            pltpu.VMEM((sections - 1, chunks, rows, width), half),
            pltpu.VMEM((chunks, rows, width), half),
            pltpu.VMEM((parts, rows, width), half),
            pltpu.VMEM((sections, parts, rows, width), half),
            pltpu.VMEM((devices, width, width), half),
            pltpu.VMEM((sections, parts, rows, width), jnp.float32),
            dma((chunks,)),
            dma((sections,)),
            dma,
            dma((chunks,)),
            dma((sections, chunks)),
            dma((sections, chunks)),
            dma((sections,)),
            dma((sections,)),
            dma((sections,)),
            dma((sections,)),
        ],
        compiler_params=pltpu.CompilerParams(
            collective_id=0, has_side_effects=True, vmem_limit_bytes=VMEM_LIMIT
        ),
        cost_estimate=pl.CostEstimate(
            flops=4 * sections * batch * columns * width,
            bytes_accessed=4 * batch * columns + 4 * sections * columns * width,
            transcendentals=0,
        ),
        name="butterfly",
    )(voxel_rows, factor_weight, extra_weight, extra_pairs, tile_owner)


def solution(mesh):
    placed = (P(None, "cols"), P(None, None, "cols", None), P("cols", None, None), P(), P())
    return jax.shard_map(
        per_device, mesh=mesh, in_specs=placed, out_specs=P(None, "cols"), check_vma=False
    )
```

```python
import functools

import jax
import jax.numpy as jnp
from jax import lax
from jax.experimental import pallas as pl
from jax.experimental.pallas import tpu as pltpu
from jax.sharding import PartitionSpec as P

MESH = pl.DeviceIdType.MESH
ROW_PARTS = 3
VMEM_LIMIT = 58 * 1024 * 1024


def butterfly_kernel(
    sections, blocks, parts,
    vox_hbm, factor_hbm, tile_hbm, pairs, owner, out_hbm,
    vox, weights, recv, hidden, result, picked, far_picked, tiles, terms,
    vox_sem, weight_sem, tile_sem, out_sem,
    send_sem, recv_sem, pick_send, pick_recv, tile_send, tile_recv,
):
    me = lax.axis_index("cols")
    chunks, rows, width = vox.shape
    bits = [lax.rem(me // 2**b, 2) for b in range(sections)]
    partners = [me + (1 - 2 * bits[b]) * 2**b for b in range(sections)]
    last = sections - 1
    pieces = [min(2 ** max(g - 1, 0), 4) for g in range(sections)]
    lag = list(range(last)) + [sum(pieces) + 1]

    def reverse(number):
        return sum(lax.rem(number // 2**b, 2) * 2 ** (last - b) for b in range(sections))

    my_place = reverse(me)

    def window(ref, c):
        row = pl.multiple_of(lax.rem(c, parts) * rows, rows)
        col = pl.multiple_of((c // parts) * width, width)
        return ref.at[pl.ds(row, rows), pl.ds(col, width)]

    def load_vox(c):
        return pltpu.make_async_copy(window(vox_hbm, c), vox.at[c], vox_sem.at[c])

    def load_weight(s):
        return pltpu.make_async_copy(factor_hbm.at[s], weights.at[s], weight_sem.at[s])

    def store_out(c):
        return pltpu.make_async_copy(result.at[c], window(out_hbm, c), out_sem.at[c])

    def send_section(s, c):
        source = vox.at[c] if s == 0 else hidden.at[s - 1, c]
        return pltpu.make_async_remote_copy(
            src_ref=source, dst_ref=recv.at[s, c],
            send_sem=send_sem.at[s, c], recv_sem=recv_sem.at[s, c],
            device_id=(partners[s],), device_id_type=MESH,
        )

    def send_picked(b, part):
        return pltpu.make_async_remote_copy(
            src_ref=picked.at[part], dst_ref=far_picked.at[b, part],
            send_sem=pick_send.at[b, part], recv_sem=pick_recv.at[b, part],
            device_id=(partners[b],), device_id_type=MESH,
        )

    def send_tiles(g, piece, arriving=False):
        start = (my_place // 2**g) * 2**g
        if arriving:
            start = start + (1 - 2 * lax.rem(my_place // 2**g, 2)) * 2**g
        count = 2**g // pieces[g]
        group = tiles.at[pl.ds(start + piece * count, count)]
        return pltpu.make_async_remote_copy(
            src_ref=group, dst_ref=group,
            send_sem=tile_send.at[g, piece], recv_sem=tile_recv.at[g, piece],
            device_id=(partners[last - g],), device_id_type=MESH,
        )

    def wait_tiles(g):
        for piece in range(pieces[g]):
            send_tiles(g, piece, arriving=True).wait_recv()

    tile_load = pltpu.make_async_copy(tile_hbm, tiles.at[pl.ds(my_place, 1)], tile_sem)
    for c in range(chunks):
        load_vox(c).start()
    tile_load.start()
    for s in range(sections):
        load_weight(s).start()

    barrier = pltpu.get_barrier_semaphore()
    for b in range(sections):
        pl.semaphore_signal(barrier, inc=1, device_id=(partners[b],), device_id_type=MESH)
    pl.semaphore_wait(barrier, sections)

    for c in range(chunks):
        load_vox(c).wait()
        send_section(0, c).start()
    offset = jnp.clip(pairs[me, 1] - me * blocks, 0, blocks - 1)
    for part in range(parts):
        picked[part] = vox[offset * parts + part]
    tile_load.wait()
    send_tiles(0, 0).start()
    for b in (last, last - 1):
        for part in range(parts):
            send_picked(b, part).start()

    pick_step = {(b, part): 2 + b + 2 * part for b in range(last - 1) for part in range(parts)}
    tile_order = [(g, piece) for g in range(1, sections) for piece in range(pieces[g])]

    def compute(s, c):
        i = c // parts
        if s == 0:
            own = vox[c]
        else:
            own = hidden[s - 1, c]
        both = jnp.concatenate([own, recv[s, c]], axis=1)
        place = pl.ds(pl.multiple_of(i * width, width), width)
        factors = jnp.concatenate([weights[s, 0, place, :], weights[s, 1, place, :]], axis=0)
        return jnp.dot(both, factors, preferred_element_type=jnp.float32)

    def step(t, carry):
        for s in range(sections):
            c = t - lag[s]

            @pl.when(c == 0)
            def _():
                load_weight(s).wait()

            if s == last:

                @pl.when(c == 0)
                def _():
                    wait_tiles(last)
                    for b in range(sections):
                        for part in range(parts):
                            send_picked(b, part).wait_recv()
                        tile = tiles[reverse(owner[partners[b]])]
                        for part in range(parts):
                            terms[b, part] = jnp.dot(
                                far_picked[b, part], tile, preferred_element_type=jnp.float32
                            )

            @pl.when((c >= 0) & (c < chunks))
            def _():
                send_section(s, c).wait_recv()
                total = compute(s, c)
                if s < last:
                    hidden[s, c] = total.astype(jnp.bfloat16)
                    send_section(s + 1, c).start()
                else:
                    for b in range(sections):
                        slot = pairs[partners[b], 0] - me * blocks
                        mask = jnp.where(slot == c // parts, jnp.float32(1), jnp.float32(0))
                        total = total + mask * terms[b, lax.rem(c, parts)]
                    result[c] = total.astype(jnp.bfloat16)
                    store_out(c).start()

        for (b, part), when in pick_step.items():

            @pl.when(t == when)
            def _():
                send_picked(b, part).start()

        for when, (g, piece) in enumerate(tile_order):

            @pl.when(t == when + 1)
            def _():
                if piece == 0:
                    wait_tiles(g - 1)
                send_tiles(g, piece).start()

        return carry

    lax.fori_loop(0, chunks + lag[last], step, 0)

    for b in range(sections):
        for part in range(parts):
            send_picked(b, part).wait_send()
        for piece in range(pieces[b]):
            send_tiles(b, piece).wait_send()

    def finish(c, carry):
        for s in range(sections):
            send_section(s, c).wait_send()
        store_out(c).wait()
        return carry

    lax.fori_loop(0, chunks, finish, 0)


def per_device(voxel_rows, factor_weight, extra_weight, extra_pairs, tile_owner):
    devices = lax.axis_size("cols")
    sections = devices.bit_length() - 1
    batch, columns = voxel_rows.shape
    width = extra_weight.shape[1]
    blocks = columns // width
    parts = ROW_PARTS
    rows = batch // parts
    chunks = blocks * parts
    half = jnp.bfloat16
    dma = pltpu.SemaphoreType.DMA
    anywhere = pl.BlockSpec(memory_space=pl.ANY)
    scalars = pl.BlockSpec(memory_space=pltpu.SMEM)
    return pl.pallas_call(
        functools.partial(butterfly_kernel, sections, blocks, parts),
        out_shape=jax.ShapeDtypeStruct(voxel_rows.shape, half),
        in_specs=[anywhere, anywhere, anywhere, scalars, scalars],
        out_specs=anywhere,
        scratch_shapes=[
            pltpu.VMEM((chunks, rows, width), half),
            pltpu.VMEM(factor_weight.shape, half),
            pltpu.VMEM((sections, chunks, rows, width), half),
            pltpu.VMEM((sections - 1, chunks, rows, width), half),
            pltpu.VMEM((chunks, rows, width), half),
            pltpu.VMEM((parts, rows, width), half),
            pltpu.VMEM((sections, parts, rows, width), half),
            pltpu.VMEM((devices, width, width), half),
            pltpu.VMEM((sections, parts, rows, width), jnp.float32),
            dma((chunks,)),
            dma((sections,)),
            dma,
            dma((chunks,)),
            dma((sections, chunks)),
            dma((sections, chunks)),
            dma((sections, parts)),
            dma((sections, parts)),
            dma((sections, 4)),
            dma((sections, 4)),
        ],
        compiler_params=pltpu.CompilerParams(
            collective_id=0, has_side_effects=True, vmem_limit_bytes=VMEM_LIMIT
        ),
        cost_estimate=pl.CostEstimate(
            flops=4 * sections * batch * columns * width,
            bytes_accessed=4 * batch * columns + 4 * sections * columns * width,
            transcendentals=0,
        ),
        name="butterfly",
    )(voxel_rows, factor_weight, extra_weight, extra_pairs, tile_owner)


def solution(mesh):
    placed = (P(None, "cols"), P(None, None, "cols", None), P("cols", None, None), P(), P())
    return jax.shard_map(
        per_device, mesh=mesh, in_specs=placed, out_specs=P(None, "cols"), check_vma=False
    )
```

```python
import functools

import jax
import jax.numpy as jnp
from jax import lax
from jax.experimental import pallas as pl
from jax.experimental.pallas import tpu as pltpu
from jax.sharding import PartitionSpec as P

MESH = pl.DeviceIdType.MESH
ROW_PARTS = 3
VMEM_LIMIT = 58 * 1024 * 1024


def butterfly_kernel(
    sections, blocks, parts,
    vox_hbm, factor_hbm, tile_hbm, pairs, owner, out_hbm,
    vox, weights, recv, hidden, result, picked, far_picked, tiles, terms,
    vox_sem, weight_sem, tile_sem, out_sem,
    send_sem, recv_sem, pick_send, pick_recv, tile_send, tile_recv,
):
    me = lax.axis_index("cols")
    chunks, rows, width = vox.shape
    bits = [lax.rem(me // 2**b, 2) for b in range(sections)]
    partners = [me + (1 - 2 * bits[b]) * 2**b for b in range(sections)]
    last = sections - 1
    pieces = [min(2 ** max(g - 1, 0), 4) for g in range(sections)]
    lag = list(range(last)) + [sum(pieces) + 1]
    hold = last + 1

    def reverse(number):
        return sum(lax.rem(number // 2**b, 2) * 2 ** (last - b) for b in range(sections))

    my_place = reverse(me)

    def window(ref, c):
        row = pl.multiple_of(lax.rem(c, parts) * rows, rows)
        col = pl.multiple_of((c // parts) * width, width)
        return ref.at[pl.ds(row, rows), pl.ds(col, width)]

    def load_vox(c):
        return pltpu.make_async_copy(window(vox_hbm, c), vox.at[c], vox_sem.at[c])

    def load_weight(s):
        return pltpu.make_async_copy(factor_hbm.at[s], weights.at[s], weight_sem.at[s])

    def store_out(c):
        return pltpu.make_async_copy(result.at[c], window(out_hbm, c), out_sem.at[c])

    def send_section(s, c):
        source = vox.at[c] if s == 0 else hidden.at[s - 1, c]
        return pltpu.make_async_remote_copy(
            src_ref=source, dst_ref=recv.at[s, c],
            send_sem=send_sem.at[s, c], recv_sem=recv_sem.at[s, c],
            device_id=(partners[s],), device_id_type=MESH,
        )

    def send_picked(b, part):
        return pltpu.make_async_remote_copy(
            src_ref=picked.at[part], dst_ref=far_picked.at[b, part],
            send_sem=pick_send.at[b, part], recv_sem=pick_recv.at[b, part],
            device_id=(partners[b],), device_id_type=MESH,
        )

    def send_tiles(g, piece, arriving=False):
        start = (my_place // 2**g) * 2**g
        if arriving:
            start = start + (1 - 2 * lax.rem(my_place // 2**g, 2)) * 2**g
        count = 2**g // pieces[g]
        group = tiles.at[pl.ds(start + piece * count, count)]
        return pltpu.make_async_remote_copy(
            src_ref=group, dst_ref=group,
            send_sem=tile_send.at[g, piece], recv_sem=tile_recv.at[g, piece],
            device_id=(partners[last - g],), device_id_type=MESH,
        )

    def wait_tiles(g):
        for piece in range(pieces[g]):
            send_tiles(g, piece, arriving=True).wait_recv()

    tile_load = pltpu.make_async_copy(tile_hbm, tiles.at[pl.ds(my_place, 1)], tile_sem)
    for c in range(chunks):
        load_vox(c).start()
    tile_load.start()
    for s in range(sections):
        load_weight(s).start()

    barrier = pltpu.get_barrier_semaphore()
    for b in range(sections):
        pl.semaphore_signal(barrier, inc=1, device_id=(partners[b],), device_id_type=MESH)
    pl.semaphore_wait(barrier, sections)

    for c in range(chunks):
        load_vox(c).wait()
        send_section(0, c).start()
    offset = jnp.clip(pairs[me, 1] - me * blocks, 0, blocks - 1)
    for part in range(parts):
        picked[part] = vox[offset * parts + part]
    tile_load.wait()
    send_tiles(0, 0).start()
    for b in (last, last - 1):
        for part in range(parts):
            send_picked(b, part).start()

    pick_step = {(b, part): 2 + b + 2 * part for b in range(last - 1) for part in range(parts)}
    tile_order = [(g, piece) for g in range(1, sections) for piece in range(pieces[g])]

    def compute(s, c):
        i = c // parts
        if s == 0:
            own = vox[c]
        else:
            own = hidden[s - 1, c]
        both = jnp.concatenate([own, recv[s, c]], axis=1)
        place = pl.ds(pl.multiple_of(i * width, width), width)
        factors = jnp.concatenate([weights[s, 0, place, :], weights[s, 1, place, :]], axis=0)
        return jnp.dot(both, factors, preferred_element_type=jnp.float32)

    def step(t, carry):
        for s in range(sections):
            c = t - lag[s]

            @pl.when(c == 0)
            def _():
                load_weight(s).wait()

            if s == last:

                @pl.when(c == 0)
                def _():
                    wait_tiles(last)
                    for b in range(sections):
                        for part in range(parts):
                            send_picked(b, part).wait_recv()
                        tile = tiles[reverse(owner[partners[b]])]
                        for part in range(parts):
                            terms[b, part] = jnp.dot(
                                far_picked[b, part], tile, preferred_element_type=jnp.float32
                            )

            @pl.when((c >= 0) & (c < chunks))
            def _():
                if s < last:
                    send_section(s, c).wait_recv()
                total = compute(s, c)
                if s < last:
                    hidden[s, c] = total.astype(jnp.bfloat16)
                    send_section(s + 1, c).start()
                else:
                    for b in range(sections):
                        slot = pairs[partners[b], 0] - me * blocks
                        mask = jnp.where(slot == c // parts, jnp.float32(1), jnp.float32(0))
                        total = total + mask * terms[b, lax.rem(c, parts)]
                    result[c] = total.astype(jnp.bfloat16)
                    store_out(c).start()

        held = t - hold

        @pl.when((held >= 0) & (held < chunks))
        def _():
            send_section(last, held).wait_recv()

        for (b, part), when in pick_step.items():

            @pl.when(t == when)
            def _():
                send_picked(b, part).start()

        for when, (g, piece) in enumerate(tile_order):

            @pl.when(t == when + 1)
            def _():
                if piece == 0:
                    wait_tiles(g - 1)
                send_tiles(g, piece).start()

        return carry

    lax.fori_loop(0, chunks + lag[last], step, 0)

    for b in range(sections):
        for part in range(parts):
            send_picked(b, part).wait_send()
        for piece in range(pieces[b]):
            send_tiles(b, piece).wait_send()

    def finish(c, carry):
        for s in range(sections):
            send_section(s, c).wait_send()
        store_out(c).wait()
        return carry

    lax.fori_loop(0, chunks, finish, 0)


def per_device(voxel_rows, factor_weight, extra_weight, extra_pairs, tile_owner):
    devices = lax.axis_size("cols")
    sections = devices.bit_length() - 1
    batch, columns = voxel_rows.shape
    width = extra_weight.shape[1]
    blocks = columns // width
    parts = ROW_PARTS
    rows = batch // parts
    chunks = blocks * parts
    half = jnp.bfloat16
    dma = pltpu.SemaphoreType.DMA
    anywhere = pl.BlockSpec(memory_space=pl.ANY)
    scalars = pl.BlockSpec(memory_space=pltpu.SMEM)
    return pl.pallas_call(
        functools.partial(butterfly_kernel, sections, blocks, parts),
        out_shape=jax.ShapeDtypeStruct(voxel_rows.shape, half),
        in_specs=[anywhere, anywhere, anywhere, scalars, scalars],
        out_specs=anywhere,
        scratch_shapes=[
            pltpu.VMEM((chunks, rows, width), half),
            pltpu.VMEM(factor_weight.shape, half),
            pltpu.VMEM((sections, chunks, rows, width), half),
            pltpu.VMEM((sections - 1, chunks, rows, width), half),
            pltpu.VMEM((chunks, rows, width), half),
            pltpu.VMEM((parts, rows, width), half),
            pltpu.VMEM((sections, parts, rows, width), half),
            pltpu.VMEM((devices, width, width), half),
            pltpu.VMEM((sections, parts, rows, width), jnp.float32),
            dma((chunks,)),
            dma((sections,)),
            dma,
            dma((chunks,)),
            dma((sections, chunks)),
            dma((sections, chunks)),
            dma((sections, parts)),
            dma((sections, parts)),
            dma((sections, 4)),
            dma((sections, 4)),
        ],
        compiler_params=pltpu.CompilerParams(
            collective_id=0, has_side_effects=True, vmem_limit_bytes=VMEM_LIMIT
        ),
        cost_estimate=pl.CostEstimate(
            flops=4 * sections * batch * columns * width,
            bytes_accessed=4 * batch * columns + 4 * sections * columns * width,
            transcendentals=0,
        ),
        name="butterfly",
    )(voxel_rows, factor_weight, extra_weight, extra_pairs, tile_owner)


def solution(mesh):
    placed = (P(None, "cols"), P(None, None, "cols", None), P("cols", None, None), P(), P())
    return jax.shard_map(
        per_device, mesh=mesh, in_specs=placed, out_specs=P(None, "cols"), check_vma=False
    )
```

```python
import functools

import jax
import jax.numpy as jnp
from jax import lax
from jax.experimental import pallas as pl
from jax.experimental.pallas import tpu as pltpu
from jax.sharding import PartitionSpec as P

MESH = pl.DeviceIdType.MESH
ROW_PARTS = 2
VMEM_LIMIT = 58 * 1024 * 1024


def butterfly_kernel(
    sections, blocks, parts,
    vox_hbm, factor_hbm, tile_hbm, pairs, owner, out_hbm,
    vox, weights, recv, hidden, result, picked, far_picked, tiles, terms,
    vox_sem, weight_sem, tile_sem, out_sem,
    send_sem, recv_sem, pick_send, pick_recv, tile_send, tile_recv,
):
    me = lax.axis_index("cols")
    chunks, rows, width = vox.shape
    bits = [lax.rem(me // 2**b, 2) for b in range(sections)]
    partners = [me + (1 - 2 * bits[b]) * 2**b for b in range(sections)]
    last = sections - 1
    pieces = [min(2 ** max(g - 1, 0), 4) for g in range(sections)]
    lag = list(range(last)) + [last + 1]
    extra_step = sum(pieces) + 1

    def reverse(number):
        return sum(lax.rem(number // 2**b, 2) * 2 ** (last - b) for b in range(sections))

    my_place = reverse(me)

    def window(ref, c):
        row = pl.multiple_of(lax.rem(c, parts) * rows, rows)
        col = pl.multiple_of((c // parts) * width, width)
        return ref.at[pl.ds(row, rows), pl.ds(col, width)]

    def load_vox(c):
        return pltpu.make_async_copy(window(vox_hbm, c), vox.at[c], vox_sem.at[c])

    def load_weight(s):
        return pltpu.make_async_copy(factor_hbm.at[s], weights.at[s], weight_sem.at[s])

    def store_out(c):
        return pltpu.make_async_copy(result.at[c], window(out_hbm, c), out_sem.at[c])

    def send_section(s, c):
        source = vox.at[c] if s == 0 else hidden.at[s - 1, c]
        return pltpu.make_async_remote_copy(
            src_ref=source, dst_ref=recv.at[s, c],
            send_sem=send_sem.at[s, c], recv_sem=recv_sem.at[s, c],
            device_id=(partners[s],), device_id_type=MESH,
        )

    def send_picked(b, part):
        return pltpu.make_async_remote_copy(
            src_ref=picked.at[part], dst_ref=far_picked.at[b, part],
            send_sem=pick_send.at[b, part], recv_sem=pick_recv.at[b, part],
            device_id=(partners[b],), device_id_type=MESH,
        )

    def send_tiles(g, piece, arriving=False):
        start = (my_place // 2**g) * 2**g
        if arriving:
            start = start + (1 - 2 * lax.rem(my_place // 2**g, 2)) * 2**g
        count = 2**g // pieces[g]
        group = tiles.at[pl.ds(start + piece * count, count)]
        return pltpu.make_async_remote_copy(
            src_ref=group, dst_ref=group,
            send_sem=tile_send.at[g, piece], recv_sem=tile_recv.at[g, piece],
            device_id=(partners[last - g],), device_id_type=MESH,
        )

    def wait_tiles(g):
        for piece in range(pieces[g]):
            send_tiles(g, piece, arriving=True).wait_recv()

    tile_load = pltpu.make_async_copy(tile_hbm, tiles.at[pl.ds(my_place, 1)], tile_sem)
    for c in range(chunks):
        load_vox(c).start()
    tile_load.start()
    for s in range(sections):
        load_weight(s).start()

    barrier = pltpu.get_barrier_semaphore()
    for b in range(sections):
        pl.semaphore_signal(barrier, inc=1, device_id=(partners[b],), device_id_type=MESH)
    pl.semaphore_wait(barrier, sections)

    for c in range(chunks):
        load_vox(c).wait()
        send_section(0, c).start()
    offset = jnp.clip(pairs[1, me] - me * blocks, 0, blocks - 1)
    for part in range(parts):
        picked[part] = vox[offset * parts + part]
    tile_load.wait()
    send_tiles(0, 0).start()
    for b in (last, last - 1):
        for part in range(parts):
            send_picked(b, part).start()

    pick_step = {(b, part): 2 + b + 2 * part for b in range(last - 1) for part in range(parts)}
    tile_order = [(g, piece) for g in range(1, sections) for piece in range(pieces[g])]

    def compute(s, c):
        i = c // parts
        if s == 0:
            own = vox[c]
        else:
            own = hidden[s - 1, c]
        both = jnp.concatenate([own, recv[s, c]], axis=1)
        place = pl.ds(pl.multiple_of(i * width, width), width)
        factors = jnp.concatenate([weights[s, 0, place, :], weights[s, 1, place, :]], axis=0)
        return jnp.dot(both, factors, preferred_element_type=jnp.float32)

    def add_extras(total, c):
        for b in range(sections):
            slot = pairs[0, partners[b]] - me * blocks
            mask = jnp.where(slot == c // parts, jnp.float32(1), jnp.float32(0))
            total = total + mask * terms[b, lax.rem(c, parts)]
        return total

    def finish_chunk(c, carry):
        result[c] = add_extras(result[c].astype(jnp.float32), c).astype(jnp.bfloat16)
        store_out(c).start()
        return carry

    def step(t, carry):
        for s in range(sections):
            c = t - lag[s]

            @pl.when(c == 0)
            def _():
                load_weight(s).wait()

            @pl.when((c >= 0) & (c < chunks))
            def _():
                send_section(s, c).wait_recv()
                total = compute(s, c).astype(jnp.bfloat16)
                if s < last:
                    hidden[s, c] = total
                    send_section(s + 1, c).start()
                else:
                    result[c] = total

        @pl.when(t == extra_step)
        def _():
            wait_tiles(last)
            for b in range(sections):
                for part in range(parts):
                    send_picked(b, part).wait_recv()
                tile = tiles[reverse(owner[partners[b]])]
                for part in range(parts):
                    terms[b, part] = jnp.dot(
                        far_picked[b, part], tile, preferred_element_type=jnp.float32
                    )
            lax.fori_loop(0, min(max(extra_step - lag[last], 0), chunks), finish_chunk, 0)

        c = t - lag[last]

        @pl.when((t >= extra_step) & (c >= 0) & (c < chunks))
        def _():
            finish_chunk(c, 0)

        for (b, part), when in pick_step.items():

            @pl.when(t == when)
            def _():
                send_picked(b, part).start()

        for when, (g, piece) in enumerate(tile_order):

            @pl.when(t == when + 1)
            def _():
                if piece == 0:
                    wait_tiles(g - 1)
                send_tiles(g, piece).start()

        return carry

    lax.fori_loop(0, max(chunks + lag[last], extra_step + 1), step, 0)

    for b in range(sections):
        for part in range(parts):
            send_picked(b, part).wait_send()
        for piece in range(pieces[b]):
            send_tiles(b, piece).wait_send()

    def finish(c, carry):
        for s in range(sections):
            send_section(s, c).wait_send()
        store_out(c).wait()
        return carry

    lax.fori_loop(0, chunks, finish, 0)


def per_device(voxel_rows, factor_weight, extra_weight, extra_pairs, tile_owner):
    devices = lax.axis_size("cols")
    sections = devices.bit_length() - 1
    batch, columns = voxel_rows.shape
    width = extra_weight.shape[1]
    blocks = columns // width
    parts = ROW_PARTS
    rows = batch // parts
    chunks = blocks * parts
    half = jnp.bfloat16
    dma = pltpu.SemaphoreType.DMA
    anywhere = pl.BlockSpec(memory_space=pl.ANY)
    scalars = pl.BlockSpec(memory_space=pltpu.SMEM)
    return pl.pallas_call(
        functools.partial(butterfly_kernel, sections, blocks, parts),
        out_shape=jax.ShapeDtypeStruct(voxel_rows.shape, half),
        in_specs=[anywhere, anywhere, anywhere, scalars, scalars],
        out_specs=anywhere,
        scratch_shapes=[
            pltpu.VMEM((chunks, rows, width), half),
            pltpu.VMEM(factor_weight.shape, half),
            pltpu.VMEM((sections, chunks, rows, width), half),
            pltpu.VMEM((sections - 1, chunks, rows, width), half),
            pltpu.VMEM((chunks, rows, width), half),
            pltpu.VMEM((parts, rows, width), half),
            pltpu.VMEM((sections, parts, rows, width), half),
            pltpu.VMEM((devices, width, width), half),
            pltpu.VMEM((sections, parts, rows, width), jnp.float32),
            dma((chunks,)),
            dma((sections,)),
            dma,
            dma((chunks,)),
            dma((sections, chunks)),
            dma((sections, chunks)),
            dma((sections, parts)),
            dma((sections, parts)),
            dma((sections, 4)),
            dma((sections, 4)),
        ],
        compiler_params=pltpu.CompilerParams(
            collective_id=0, has_side_effects=True, vmem_limit_bytes=VMEM_LIMIT
        ),
        cost_estimate=pl.CostEstimate(
            flops=4 * sections * batch * columns * width,
            bytes_accessed=4 * batch * columns + 4 * sections * columns * width,
            transcendentals=0,
        ),
        name="butterfly",
    )(voxel_rows, factor_weight, extra_weight, extra_pairs.T, tile_owner)


def solution(mesh):
    placed = (P(None, "cols"), P(None, None, "cols", None), P("cols", None, None), P(), P())
    return jax.shard_map(
        per_device, mesh=mesh, in_specs=placed, out_specs=P(None, "cols"), check_vma=False
    )
```

```python
import functools

import jax
import jax.numpy as jnp
from jax import lax
from jax.experimental import pallas as pl
from jax.experimental.pallas import tpu as pltpu
from jax.sharding import PartitionSpec as P

MESH = pl.DeviceIdType.MESH
ROW_PARTS = 2
VMEM_LIMIT = 58 * 1024 * 1024


def butterfly_kernel(
    sections, blocks, parts,
    vox_hbm, factor_hbm, tile_hbm, pairs, owner, out,
    vox, weights, recv, hidden, picked, far_picked, tiles, terms,
    vox_sem, weight_sem, tile_sem,
    send_sem, recv_sem, pick_send, pick_recv, tile_send, tile_recv,
):
    me = lax.axis_index("cols")
    chunks, rows, width = vox.shape
    bits = [lax.rem(me // 2**b, 2) for b in range(sections)]
    partners = [me + (1 - 2 * bits[b]) * 2**b for b in range(sections)]
    last = sections - 1
    pieces = [min(2 ** max(g - 1, 0), 4) for g in range(sections)]
    lag = list(range(last)) + [last + 1]
    extra_step = sum(pieces) + 1

    def reverse(number):
        return sum(lax.rem(number // 2**b, 2) * 2 ** (last - b) for b in range(sections))

    my_place = reverse(me)

    def window(ref, c):
        row = pl.multiple_of(lax.rem(c, parts) * rows, rows)
        col = pl.multiple_of((c // parts) * width, width)
        return ref.at[pl.ds(row, rows), pl.ds(col, width)]

    def load_vox(c):
        return pltpu.make_async_copy(window(vox_hbm, c), vox.at[c], vox_sem.at[c])

    def load_weight(s):
        return pltpu.make_async_copy(factor_hbm.at[s], weights.at[s], weight_sem.at[s])

    def send_section(s, c):
        source = vox.at[c] if s == 0 else hidden.at[s - 1, c]
        return pltpu.make_async_remote_copy(
            src_ref=source, dst_ref=recv.at[s, c],
            send_sem=send_sem.at[s, c], recv_sem=recv_sem.at[s, c],
            device_id=(partners[s],), device_id_type=MESH,
        )

    def send_picked(b, part):
        return pltpu.make_async_remote_copy(
            src_ref=picked.at[part], dst_ref=far_picked.at[b, part],
            send_sem=pick_send.at[b, part], recv_sem=pick_recv.at[b, part],
            device_id=(partners[b],), device_id_type=MESH,
        )

    def send_tiles(g, piece, arriving=False):
        start = (my_place // 2**g) * 2**g
        if arriving:
            start = start + (1 - 2 * lax.rem(my_place // 2**g, 2)) * 2**g
        count = 2**g // pieces[g]
        group = tiles.at[pl.ds(start + piece * count, count)]
        return pltpu.make_async_remote_copy(
            src_ref=group, dst_ref=group,
            send_sem=tile_send.at[g, piece], recv_sem=tile_recv.at[g, piece],
            device_id=(partners[last - g],), device_id_type=MESH,
        )

    def wait_tiles(g):
        for piece in range(pieces[g]):
            send_tiles(g, piece, arriving=True).wait_recv()

    tile_load = pltpu.make_async_copy(tile_hbm, tiles.at[pl.ds(my_place, 1)], tile_sem)
    for c in range(chunks):
        load_vox(c).start()
    tile_load.start()
    for s in range(sections):
        load_weight(s).start()

    barrier = pltpu.get_barrier_semaphore()
    for b in range(sections):
        pl.semaphore_signal(barrier, inc=1, device_id=(partners[b],), device_id_type=MESH)
    pl.semaphore_wait(barrier, sections)

    for c in range(chunks):
        load_vox(c).wait()
        send_section(0, c).start()
    offset = jnp.clip(pairs[1, me] - me * blocks, 0, blocks - 1)
    for part in range(parts):
        picked[part] = vox[offset * parts + part]
    tile_load.wait()
    send_tiles(0, 0).start()
    for b in (last, last - 1):
        for part in range(parts):
            send_picked(b, part).start()

    pick_step = {(b, part): 2 + b + 2 * part for b in range(last - 1) for part in range(parts)}
    tile_order = [(g, piece) for g in range(1, sections) for piece in range(pieces[g])]

    def compute(s, c):
        i = c // parts
        if s == 0:
            own = vox[c]
        else:
            own = hidden[s - 1, c]
        both = jnp.concatenate([own, recv[s, c]], axis=1)
        place = pl.ds(pl.multiple_of(i * width, width), width)
        factors = jnp.concatenate([weights[s, 0, place, :], weights[s, 1, place, :]], axis=0)
        return jnp.dot(both, factors, preferred_element_type=jnp.float32)

    def add_extras(total, c):
        for b in range(sections):
            slot = pairs[0, partners[b]] - me * blocks
            mask = jnp.where(slot == c // parts, jnp.float32(1), jnp.float32(0))
            total = total + mask * terms[b, lax.rem(c, parts)]
        return total

    def finish_chunk(c, carry):
        place = window(out, c)
        place[...] = add_extras(place[...].astype(jnp.float32), c).astype(jnp.bfloat16)
        return carry

    def step(t, carry):
        for s in range(sections):
            c = t - lag[s]

            @pl.when(c == 0)
            def _():
                load_weight(s).wait()

            @pl.when((c >= 0) & (c < chunks))
            def _():
                send_section(s, c).wait_recv()
                total = compute(s, c).astype(jnp.bfloat16)
                if s < last:
                    hidden[s, c] = total
                    send_section(s + 1, c).start()
                else:
                    window(out, c)[...] = total

        @pl.when(t == extra_step)
        def _():
            wait_tiles(last)
            for b in range(sections):
                for part in range(parts):
                    send_picked(b, part).wait_recv()
                tile = tiles[reverse(owner[partners[b]])]
                for part in range(parts):
                    terms[b, part] = jnp.dot(
                        far_picked[b, part], tile, preferred_element_type=jnp.float32
                    )
            lax.fori_loop(0, min(max(extra_step - lag[last], 0), chunks), finish_chunk, 0)

        c = t - lag[last]

        @pl.when((t >= extra_step) & (c >= 0) & (c < chunks))
        def _():
            finish_chunk(c, 0)

        for (b, part), when in pick_step.items():

            @pl.when(t == when)
            def _():
                send_picked(b, part).start()

        for when, (g, piece) in enumerate(tile_order):

            @pl.when(t == when + 1)
            def _():
                if piece == 0:
                    wait_tiles(g - 1)
                send_tiles(g, piece).start()

        return carry

    lax.fori_loop(0, max(chunks + lag[last], extra_step + 1), step, 0)

    for b in range(sections):
        for part in range(parts):
            send_picked(b, part).wait_send()
        for piece in range(pieces[b]):
            send_tiles(b, piece).wait_send()

    def finish(c, carry):
        for s in range(sections):
            send_section(s, c).wait_send()
        return carry

    lax.fori_loop(0, chunks, finish, 0)


def per_device(voxel_rows, factor_weight, extra_weight, extra_pairs, tile_owner):
    devices = lax.axis_size("cols")
    sections = devices.bit_length() - 1
    batch, columns = voxel_rows.shape
    width = extra_weight.shape[1]
    blocks = columns // width
    parts = ROW_PARTS
    rows = batch // parts
    chunks = blocks * parts
    half = jnp.bfloat16
    dma = pltpu.SemaphoreType.DMA
    in_hbm = pl.BlockSpec(memory_space=pltpu.HBM)
    scalars = pl.BlockSpec(memory_space=pltpu.SMEM)
    return pl.pallas_call(
        functools.partial(butterfly_kernel, sections, blocks, parts),
        out_shape=pltpu.VMEM(voxel_rows.shape, half),
        in_specs=[in_hbm, in_hbm, in_hbm, scalars, scalars],
        out_specs=pl.BlockSpec(memory_space=pltpu.VMEM),
        scratch_shapes=[
            pltpu.VMEM((chunks, rows, width), half),
            pltpu.VMEM(factor_weight.shape, half),
            pltpu.VMEM((sections, chunks, rows, width), half),
            pltpu.VMEM((sections - 1, chunks, rows, width), half),
            pltpu.VMEM((parts, rows, width), half),
            pltpu.VMEM((sections, parts, rows, width), half),
            pltpu.VMEM((devices, width, width), half),
            pltpu.VMEM((sections, parts, rows, width), jnp.float32),
            dma((chunks,)),
            dma((sections,)),
            dma,
            dma((sections, chunks)),
            dma((sections, chunks)),
            dma((sections, parts)),
            dma((sections, parts)),
            dma((sections, 4)),
            dma((sections, 4)),
        ],
        compiler_params=pltpu.CompilerParams(
            collective_id=0, has_side_effects=True, vmem_limit_bytes=VMEM_LIMIT
        ),
        cost_estimate=pl.CostEstimate(
            flops=4 * sections * batch * columns * width,
            bytes_accessed=4 * batch * columns + 4 * sections * columns * width,
            transcendentals=0,
        ),
        name="butterfly",
    )(voxel_rows, factor_weight, extra_weight, extra_pairs.T, tile_owner)


def solution(mesh):
    placed = (P(None, "cols"), P(None, None, "cols", None), P("cols", None, None), P(), P())
    return jax.shard_map(
        per_device, mesh=mesh, in_specs=placed, out_specs=P(None, "cols"), check_vma=False
    )
```

```python
import functools

import jax
import jax.numpy as jnp
from jax import lax
from jax.experimental import pallas as pl
from jax.experimental.pallas import tpu as pltpu
from jax.sharding import PartitionSpec as P

MESH = pl.DeviceIdType.MESH
ROW_PARTS = 2
MIX_STEPS = 2
END_STEPS = 2
WEIGHT_LEAD = 2
VMEM_LIMIT = 58 * 1024 * 1024


def butterfly_kernel(
    sections, blocks, parts,
    vox_hbm, factor_hbm, tile_hbm, pairs, owner, out,
    vox, weights, recv, hidden, mixed, far_mixed, ended, far_ended, far_weights,
    picked, far_picked, tiles, terms,
    vox_sem, weight_sem, tile_sem,
    send_sem, recv_sem, mix_send, mix_recv, end_send, end_recv, far_send, far_recv,
    pick_send, pick_recv, tile_send, tile_recv,
):
    me = lax.axis_index("cols")
    chunks, rows, width = vox.shape
    bits = [lax.rem(me // 2**b, 2) for b in range(sections)]
    partners = [me + (1 - 2 * bits[b]) * 2**b for b in range(sections)]
    last = sections - 1
    near = last - 1
    spot = me // 2**near
    inner = (spot == 1) | (spot == 2)
    outer = (spot == 0) | (spot == 3)
    mirror = me + (3 - 2 * spot) * 2**near
    pieces = [min(2 ** max(g - 1, 0), 4) for g in range(sections)]
    mix_lag, join_lag, end_lag = near, near + MIX_STEPS, near + MIX_STEPS + END_STEPS
    extra_step = sum(pieces) + 1

    def reverse(number):
        return sum(lax.rem(number // 2**b, 2) * 2 ** (last - b) for b in range(sections))

    my_place = reverse(me)

    def window(ref, c):
        row = pl.multiple_of(lax.rem(c, parts) * rows, rows)
        col = pl.multiple_of((c // parts) * width, width)
        return ref.at[pl.ds(row, rows), pl.ds(col, width)]

    def load_vox(c):
        return pltpu.make_async_copy(window(vox_hbm, c), vox.at[c], vox_sem.at[c])

    def load_weight(s):
        return pltpu.make_async_copy(factor_hbm.at[s], weights.at[s], weight_sem.at[s])

    def send_section(s, c):
        source = vox.at[c] if s == 0 else hidden.at[s - 1, c]
        return pltpu.make_async_remote_copy(
            src_ref=source, dst_ref=recv.at[s, c],
            send_sem=send_sem.at[s, c], recv_sem=recv_sem.at[s, c],
            device_id=(partners[s],), device_id_type=MESH,
        )

    def send_mixed(c):
        return pltpu.make_async_remote_copy(
            src_ref=mixed.at[c], dst_ref=far_mixed.at[c],
            send_sem=mix_send.at[c], recv_sem=mix_recv.at[c],
            device_id=(mirror,), device_id_type=MESH,
        )

    def send_ended(c):
        return pltpu.make_async_remote_copy(
            src_ref=ended.at[c], dst_ref=far_ended.at[c],
            send_sem=end_send.at[c], recv_sem=end_recv.at[c],
            device_id=(partners[near],), device_id_type=MESH,
        )

    def block_rows(i):
        return pl.ds(pl.multiple_of(i * width, width), width)

    def send_weight(which, i):
        return pltpu.make_async_remote_copy(
            src_ref=weights.at[near + which, :, block_rows(i)],
            dst_ref=far_weights.at[which, :, block_rows(i)],
            send_sem=far_send.at[which, i], recv_sem=far_recv.at[which, i],
            device_id=(partners[near],), device_id_type=MESH,
        )

    def send_picked(b, part):
        return pltpu.make_async_remote_copy(
            src_ref=picked.at[part], dst_ref=far_picked.at[b, part],
            send_sem=pick_send.at[b, part], recv_sem=pick_recv.at[b, part],
            device_id=(partners[b],), device_id_type=MESH,
        )

    def send_tiles(g, piece, arriving=False):
        start = (my_place // 2**g) * 2**g
        if arriving:
            start = start + (1 - 2 * lax.rem(my_place // 2**g, 2)) * 2**g
        count = 2**g // pieces[g]
        group = tiles.at[pl.ds(start + piece * count, count)]
        return pltpu.make_async_remote_copy(
            src_ref=group, dst_ref=group,
            send_sem=tile_send.at[g, piece], recv_sem=tile_recv.at[g, piece],
            device_id=(partners[last - g],), device_id_type=MESH,
        )

    def wait_tiles(g):
        for piece in range(pieces[g]):
            send_tiles(g, piece, arriving=True).wait_recv()

    tile_load = pltpu.make_async_copy(tile_hbm, tiles.at[pl.ds(my_place, 1)], tile_sem)
    for c in range(chunks):
        load_vox(c).start()
    tile_load.start()
    for s in range(sections):
        load_weight(s).start()

    barrier = pltpu.get_barrier_semaphore()
    for b in range(sections):
        pl.semaphore_signal(barrier, inc=1, device_id=(partners[b],), device_id_type=MESH)
    pl.semaphore_signal(barrier, inc=1, device_id=(mirror,), device_id_type=MESH)
    pl.semaphore_wait(barrier, sections + 1)

    for c in range(chunks):
        load_vox(c).wait()
        send_section(0, c).start()
    offset = jnp.clip(pairs[1, me] - me * blocks, 0, blocks - 1)
    for part in range(parts):
        picked[part] = vox[offset * parts + part]
    tile_load.wait()
    send_tiles(0, 0).start()
    for part in range(parts):
        send_picked(last, part).start()
    load_weight(near).wait()
    load_weight(last).wait()

    @pl.when(outer)
    def _():
        for i in range(min(WEIGHT_LEAD, blocks)):
            send_weight(0, i).start()
            send_weight(1, i).start()

    pick_step = {(b, part): 2 + b + 2 * part for b in range(last) for part in range(parts)}
    tile_order = [(g, piece) for g in range(1, sections) for piece in range(pieces[g])]

    def mix(own, other, factors, c):
        place = block_rows(c // parts)
        both = jnp.concatenate([own, other], axis=1)
        stack = jnp.concatenate([factors[0, place, :], factors[1, place, :]], axis=0)
        total = jnp.dot(both, stack, preferred_element_type=jnp.float32)
        return total.astype(jnp.bfloat16)

    def add_extras(total, c):
        for b in range(sections):
            slot = pairs[0, partners[b]] - me * blocks
            mask = jnp.where(slot == c // parts, jnp.float32(1), jnp.float32(0))
            total = total + mask * terms[b, lax.rem(c, parts)]
        return total

    def finish_chunk(c, carry):
        place = window(out, c)
        place[...] = add_extras(place[...].astype(jnp.float32), c).astype(jnp.bfloat16)
        return carry

    def step(t, carry):
        for s in range(near):
            c = t - s

            @pl.when(c == 0)
            def _():
                load_weight(s).wait()

            @pl.when((c >= 0) & (c < chunks))
            def _():
                send_section(s, c).wait_recv()
                own = vox[c] if s == 0 else hidden[s - 1, c]
                hidden[s, c] = mix(own, recv[s, c], weights.at[s], c)
                if s < near - 1:
                    send_section(s + 1, c).start()
                else:

                    @pl.when(outer)
                    def _():
                        send_section(near, c).start()

        c_mix = t - mix_lag

        @pl.when(inner & (c_mix >= 0) & (c_mix < chunks))
        def _():
            c = c_mix
            send_section(near, c).wait_recv()

            @pl.when(lax.rem(c, parts) == 0)
            def _():
                send_weight(0, c // parts).wait_recv()

            own, other = hidden[near - 1, c], recv[near, c]
            mixed[c, 0] = mix(own, other, weights.at[near], c)
            mixed[c, 1] = mix(other, own, far_weights.at[0], c)
            send_mixed(c).start()

        c_join = t - join_lag

        @pl.when(inner & (c_join >= 0) & (c_join < chunks))
        def _():
            c = c_join
            send_mixed(c).wait_recv()

            @pl.when(lax.rem(c, parts) == 0)
            def _():
                send_weight(1, c // parts).wait_recv()

            ended[c] = mix(mixed[c, 1], far_mixed[c, 0], far_weights.at[1], c)
            send_ended(c).start()
            window(out, c)[...] = mix(mixed[c, 0], far_mixed[c, 1], weights.at[last], c)

        c_end = t - end_lag

        @pl.when(outer & (c_end >= 0) & (c_end < chunks))
        def _():
            send_ended(c_end).wait_recv()
            window(out, c_end)[...] = far_ended[c_end]

        ahead = t // 2 + WEIGHT_LEAD
        for which in range(2):

            @pl.when(outer & (lax.rem(t, 2) == which) & (ahead < blocks))
            def _():
                send_weight(which, ahead).start()

        @pl.when(t == extra_step)
        def _():
            wait_tiles(last)
            for b in range(sections):
                for part in range(parts):
                    send_picked(b, part).wait_recv()
                tile = tiles[reverse(owner[partners[b]])]
                for part in range(parts):
                    terms[b, part] = jnp.dot(
                        far_picked[b, part], tile, preferred_element_type=jnp.float32
                    )
            for role, lag in ((inner, join_lag), (outer, end_lag)):

                @pl.when(role)
                def _():
                    lax.fori_loop(0, min(max(extra_step - lag, 0), chunks), finish_chunk, 0)

        for role, c in ((inner, c_join), (outer, c_end)):

            @pl.when(role & (t >= extra_step) & (c >= 0) & (c < chunks))
            def _():
                finish_chunk(c, 0)

        for (b, part), when in pick_step.items():

            @pl.when(t == when)
            def _():
                send_picked(b, part).start()

        for when, (g, piece) in enumerate(tile_order):

            @pl.when(t == when + 1)
            def _():
                if piece == 0:
                    wait_tiles(g - 1)
                send_tiles(g, piece).start()

        return carry

    lax.fori_loop(0, max(chunks + end_lag, extra_step + 1), step, 0)

    for b in range(sections):
        for part in range(parts):
            send_picked(b, part).wait_send()
        for piece in range(pieces[b]):
            send_tiles(b, piece).wait_send()

    def finish(c, carry):
        for s in range(near):
            send_section(s, c).wait_send()

        @pl.when(outer)
        def _():
            send_section(near, c).wait_send()

        @pl.when(inner)
        def _():
            send_mixed(c).wait_send()
            send_ended(c).wait_send()

        return carry

    @pl.when(outer)
    def _():
        for i in range(blocks):
            send_weight(0, i).wait_send()
            send_weight(1, i).wait_send()

    lax.fori_loop(0, chunks, finish, 0)


def per_device(voxel_rows, factor_weight, extra_weight, extra_pairs, tile_owner):
    devices = lax.axis_size("cols")
    sections = devices.bit_length() - 1
    batch, columns = voxel_rows.shape
    width = extra_weight.shape[1]
    blocks = columns // width
    parts = ROW_PARTS
    rows = batch // parts
    chunks = blocks * parts
    half = jnp.bfloat16
    dma = pltpu.SemaphoreType.DMA
    in_hbm = pl.BlockSpec(memory_space=pltpu.HBM)
    scalars = pl.BlockSpec(memory_space=pltpu.SMEM)
    return pl.pallas_call(
        functools.partial(butterfly_kernel, sections, blocks, parts),
        out_shape=pltpu.VMEM(voxel_rows.shape, half),
        in_specs=[in_hbm, in_hbm, in_hbm, scalars, scalars],
        out_specs=pl.BlockSpec(memory_space=pltpu.VMEM),
        scratch_shapes=[
            pltpu.VMEM((chunks, rows, width), half),
            pltpu.VMEM(factor_weight.shape, half),
            pltpu.VMEM((sections - 1, chunks, rows, width), half),
            pltpu.VMEM((sections - 2, chunks, rows, width), half),
            pltpu.VMEM((chunks, 2, rows, width), half),
            pltpu.VMEM((chunks, 2, rows, width), half),
            pltpu.VMEM((chunks, rows, width), half),
            pltpu.VMEM((chunks, rows, width), half),
            pltpu.VMEM((2,) + factor_weight.shape[1:], half),
            pltpu.VMEM((parts, rows, width), half),
            pltpu.VMEM((sections, parts, rows, width), half),
            pltpu.VMEM((devices, width, width), half),
            pltpu.VMEM((sections, parts, rows, width), jnp.float32),
            dma((chunks,)),
            dma((sections,)),
            dma,
            dma((sections - 1, chunks)),
            dma((sections - 1, chunks)),
            dma((chunks,)),
            dma((chunks,)),
            dma((chunks,)),
            dma((chunks,)),
            dma((2, blocks)),
            dma((2, blocks)),
            dma((sections, parts)),
            dma((sections, parts)),
            dma((sections, 4)),
            dma((sections, 4)),
        ],
        compiler_params=pltpu.CompilerParams(
            collective_id=0, has_side_effects=True, vmem_limit_bytes=VMEM_LIMIT
        ),
        cost_estimate=pl.CostEstimate(
            flops=4 * sections * batch * columns * width,
            bytes_accessed=4 * batch * columns + 4 * sections * columns * width,
            transcendentals=0,
        ),
        name="butterfly",
    )(voxel_rows, factor_weight, extra_weight, extra_pairs.T, tile_owner)


def solution(mesh):
    placed = (P(None, "cols"), P(None, None, "cols", None), P("cols", None, None), P(), P())
    return jax.shard_map(
        per_device, mesh=mesh, in_specs=placed, out_specs=P(None, "cols"), check_vma=False
    )
```

```python
import functools

import jax
import jax.numpy as jnp
from jax import lax
from jax.experimental import pallas as pl
from jax.experimental.pallas import tpu as pltpu
from jax.sharding import PartitionSpec as P

MESH = pl.DeviceIdType.MESH
VMEM_LIMIT = 58 * 1024 * 1024


def butterfly_kernel(
    sections, chunk_table,
    vox_hbm, factor_hbm, tile_hbm, pairs, owner, out,
    vox, weights, recv, hidden, picked, far_picked, tiles, terms,
    vox_sem, weight_sem, tile_sem,
    send_sem, recv_sem, pick_send, pick_recv, tile_send, tile_recv,
):
    me = lax.axis_index("cols")
    blocks, batch, width = vox.shape
    lead, chunks = chunk_table
    parts, half_rows = 2, batch // 2
    bits = [lax.rem(me // 2**b, 2) for b in range(sections)]
    partners = [me + (1 - 2 * bits[b]) * 2**b for b in range(sections)]
    last = sections - 1
    pieces = [min(2 ** max(g - 1, 0), 4) for g in range(sections)]
    lag = list(range(last)) + [last + 1]
    extra_step = sum(pieces) + 1

    def reverse(number):
        return sum(lax.rem(number // 2**b, 2) * 2 ** (last - b) for b in range(sections))

    my_place = reverse(me)

    def spot(c):
        if isinstance(c, int) and c < len(lead):
            return 0, sum(lead[:c]), lead[c]
        later = c - len(lead)
        block, part = 1 + later // parts, later % parts
        return block, part * half_rows, half_rows

    def window(ref, c):
        block, row, rows = spot(c)
        if not isinstance(c, int):
            row = pl.multiple_of(row, half_rows)
            block = pl.multiple_of(block * width, width)
        else:
            block = block * width
        return ref.at[pl.ds(row, rows), pl.ds(block, width)]

    def piece_of(ref, c):
        block, row, rows = spot(c)
        if not isinstance(c, int):
            row = pl.multiple_of(row, half_rows)
        return ref.at[block, pl.ds(row, rows)]

    def load_vox(c):
        return pltpu.make_async_copy(window(vox_hbm, c), piece_of(vox, c), vox_sem.at[c])

    def load_weight(s):
        return pltpu.make_async_copy(factor_hbm.at[s], weights.at[s], weight_sem.at[s])

    def send_section(s, c):
        source = vox if s == 0 else hidden.at[s - 1]
        return pltpu.make_async_remote_copy(
            src_ref=piece_of(source, c), dst_ref=piece_of(recv.at[s], c),
            send_sem=send_sem.at[s, c], recv_sem=recv_sem.at[s, c],
            device_id=(partners[s],), device_id_type=MESH,
        )

    def half_of(ref, part):
        return ref.at[pl.ds(part * half_rows, half_rows)]

    def send_picked(b, part):
        return pltpu.make_async_remote_copy(
            src_ref=half_of(picked, part), dst_ref=half_of(far_picked.at[b], part),
            send_sem=pick_send.at[b, part], recv_sem=pick_recv.at[b, part],
            device_id=(partners[b],), device_id_type=MESH,
        )

    def send_tiles(g, piece, arriving=False):
        start = (my_place // 2**g) * 2**g
        if arriving:
            start = start + (1 - 2 * lax.rem(my_place // 2**g, 2)) * 2**g
        count = 2**g // pieces[g]
        group = tiles.at[pl.ds(start + piece * count, count)]
        return pltpu.make_async_remote_copy(
            src_ref=group, dst_ref=group,
            send_sem=tile_send.at[g, piece], recv_sem=tile_recv.at[g, piece],
            device_id=(partners[last - g],), device_id_type=MESH,
        )

    def wait_tiles(g):
        for piece in range(pieces[g]):
            send_tiles(g, piece, arriving=True).wait_recv()

    tile_load = pltpu.make_async_copy(tile_hbm, tiles.at[pl.ds(my_place, 1)], tile_sem)
    for c in range(chunks):
        load_vox(c).start()
    tile_load.start()
    for s in range(sections):
        load_weight(s).start()

    barrier = pltpu.get_barrier_semaphore()
    for b in range(sections):
        pl.semaphore_signal(barrier, inc=1, device_id=(partners[b],), device_id_type=MESH)
    pl.semaphore_wait(barrier, sections)

    for c in range(chunks):
        load_vox(c).wait()
        send_section(0, c).start()
    offset = jnp.clip(pairs[1, me] - me * blocks, 0, blocks - 1)
    picked[...] = vox[offset]
    tile_load.wait()
    send_tiles(0, 0).start()
    for b in (last, last - 1):
        for part in range(parts):
            send_picked(b, part).start()

    pick_step = {(b, part): 6 + b + 2 * part for b in range(last - 1) for part in range(parts)}
    tile_order = [(g, piece) for g in range(1, sections) for piece in range(pieces[g])]

    def run_if(condition, action):
        if isinstance(condition, bool):
            if condition:
                action()
        else:
            pl.when(condition)(action)

    def mix(s, c):
        block = spot(c)[0]
        own = piece_of(vox if s == 0 else hidden.at[s - 1], c)
        both = jnp.concatenate([own[...], piece_of(recv.at[s], c)[...]], axis=1)
        place = block * width
        if not isinstance(c, int):
            place = pl.multiple_of(place, width)
        place = pl.ds(place, width)
        factors = jnp.concatenate([weights[s, 0, place, :], weights[s, 1, place, :]], axis=0)
        total = jnp.dot(both, factors, preferred_element_type=jnp.float32)
        return total.astype(jnp.bfloat16)

    def finish_chunk(c):
        block, row, rows = spot(c)
        if not isinstance(c, int):
            row = pl.multiple_of(row, half_rows)
        place = window(out, c)
        total = place[...].astype(jnp.float32)
        for b in range(sections):
            slot = pairs[0, partners[b]] - me * blocks
            mask = jnp.where(slot == block, jnp.float32(1), jnp.float32(0))
            total = total + mask * terms[b, pl.ds(row, rows), :]
        place[...] = total.astype(jnp.bfloat16)

    def start_extras():
        wait_tiles(last)
        for b in range(sections):
            for part in range(parts):
                send_picked(b, part).wait_recv()
            tile = tiles[reverse(owner[partners[b]])]
            terms[b] = jnp.dot(far_picked[b], tile, preferred_element_type=jnp.float32)
        done = min(max(extra_step - lag[last], 0), chunks)
        for c in range(min(done, len(lead))):
            finish_chunk(c)

        def finish_late(c, carry):
            finish_chunk(c)
            return carry

        lax.fori_loop(len(lead), max(done, len(lead)), finish_late, 0)

    def section_step(s, c):
        if isinstance(c, int) and c == 0:
            load_weight(s).wait()
        send_section(s, c).wait_recv()
        total = mix(s, c)
        if s < last:
            piece_of(hidden.at[s], c)[...] = total
            send_section(s + 1, c).start()
        else:
            window(out, c)[...] = total

    def tile_piece(g, piece):
        if piece == 0:
            wait_tiles(g - 1)
        send_tiles(g, piece).start()

    def step(t):
        for s in range(sections):
            c = t - lag[s]
            if isinstance(c, int):
                run_if(0 <= c < chunks, lambda: section_step(s, c))
            else:
                run_if(c < chunks, lambda: section_step(s, c))
        run_if(t == extra_step, start_extras)
        c = t - lag[last]
        if not isinstance(c, int):
            run_if((t >= extra_step) & (c < chunks), lambda: finish_chunk(c))
        for (b, part), when in pick_step.items():
            run_if(t == when, lambda: send_picked(b, part).start())
        for when, (g, piece) in enumerate(tile_order):
            run_if(t == when + 1, lambda: tile_piece(g, piece))

    def late_step(t, carry):
        step(t)
        return carry

    early = len(lead) + lag[last]
    assert early <= extra_step
    for t in range(early):
        step(t)
    lax.fori_loop(early, max(chunks + lag[last], extra_step + 1), late_step, 0)

    for b in range(sections):
        for part in range(parts):
            send_picked(b, part).wait_send()
        for piece in range(pieces[b]):
            send_tiles(b, piece).wait_send()

    def drain(c, carry=0):
        for s in range(sections):
            send_section(s, c).wait_send()
        return carry

    for c in range(len(lead)):
        drain(c)
    lax.fori_loop(len(lead), chunks, drain, 0)


def per_device(voxel_rows, factor_weight, extra_weight, extra_pairs, tile_owner):
    devices = lax.axis_size("cols")
    sections = devices.bit_length() - 1
    batch, columns = voxel_rows.shape
    width = extra_weight.shape[1]
    blocks = columns // width
    parts = 2
    lead = (batch // 8, batch // 8, batch // 4, batch // 2)
    chunks = len(lead) + (blocks - 1) * parts
    half = jnp.bfloat16
    dma = pltpu.SemaphoreType.DMA
    in_hbm = pl.BlockSpec(memory_space=pltpu.HBM)
    scalars = pl.BlockSpec(memory_space=pltpu.SMEM)
    return pl.pallas_call(
        functools.partial(butterfly_kernel, sections, (lead, chunks)),
        out_shape=pltpu.VMEM(voxel_rows.shape, half),
        in_specs=[in_hbm, in_hbm, in_hbm, scalars, scalars],
        out_specs=pl.BlockSpec(memory_space=pltpu.VMEM),
        scratch_shapes=[
            pltpu.VMEM((blocks, batch, width), half),
            pltpu.VMEM(factor_weight.shape, half),
            pltpu.VMEM((sections, blocks, batch, width), half),
            pltpu.VMEM((sections - 1, blocks, batch, width), half),
            pltpu.VMEM((batch, width), half),
            pltpu.VMEM((sections, batch, width), half),
            pltpu.VMEM((devices, width, width), half),
            pltpu.VMEM((sections, batch, width), jnp.float32),
            dma((chunks,)),
            dma((sections,)),
            dma,
            dma((sections, chunks)),
            dma((sections, chunks)),
            dma((sections, parts)),
            dma((sections, parts)),
            dma((sections, 4)),
            dma((sections, 4)),
        ],
        compiler_params=pltpu.CompilerParams(
            collective_id=0, has_side_effects=True, vmem_limit_bytes=VMEM_LIMIT
        ),
        cost_estimate=pl.CostEstimate(
            flops=4 * sections * batch * columns * width,
            bytes_accessed=4 * batch * columns + 4 * sections * columns * width,
            transcendentals=0,
        ),
        name="butterfly",
    )(voxel_rows, factor_weight, extra_weight, extra_pairs.T, tile_owner)


def solution(mesh):
    placed = (P(None, "cols"), P(None, None, "cols", None), P("cols", None, None), P(), P())
    return jax.shard_map(
        per_device, mesh=mesh, in_specs=placed, out_specs=P(None, "cols"), check_vma=False
    )
```

```python
import functools

import jax
import jax.numpy as jnp
from jax import lax
from jax.experimental import pallas as pl
from jax.experimental.pallas import tpu as pltpu
from jax.sharding import PartitionSpec as P

MESH = pl.DeviceIdType.MESH
ROW_PARTS = 2
VMEM_LIMIT = 58 * 1024 * 1024


def butterfly_kernel(
    sections, blocks, parts,
    vox_hbm, factor_hbm, tile_hbm, pairs, owner, out,
    acts, weights, recv, picked, far_picked, tiles, terms,
    vox_sem, weight_sem, tile_sem,
    send_sem, recv_sem, pick_send, pick_recv, tile_send, tile_recv,
):
    me = lax.axis_index("cols")
    _, chunks, rows, width = acts.shape
    bits = [lax.rem(me // 2**b, 2) for b in range(sections)]
    partners = [me + (1 - 2 * bits[b]) * 2**b for b in range(sections)]
    last = sections - 1
    pieces = [min(2 ** max(g - 1, 0), 4) for g in range(sections)]
    extra_step = sum(pieces) + 1

    def reverse(number):
        return sum(lax.rem(number // 2**b, 2) * 2 ** (last - b) for b in range(sections))

    my_place = reverse(me)

    def window(ref, c):
        row = pl.multiple_of(lax.rem(c, parts) * rows, rows)
        col = pl.multiple_of((c // parts) * width, width)
        return ref.at[pl.ds(row, rows), pl.ds(col, width)]

    def load_vox(c):
        return pltpu.make_async_copy(window(vox_hbm, c), acts.at[0, c], vox_sem.at[c])

    def load_weight(s):
        return pltpu.make_async_copy(factor_hbm.at[s], weights.at[s], weight_sem.at[s])

    def send_section(s, c, stride):
        partner = me + (1 - 2 * lax.rem(me // stride, 2)) * stride
        return pltpu.make_async_remote_copy(
            src_ref=acts.at[s, c], dst_ref=recv.at[s, c],
            send_sem=send_sem.at[s, c], recv_sem=recv_sem.at[s, c],
            device_id=(partner,), device_id_type=MESH,
        )

    def send_picked(b, part):
        return pltpu.make_async_remote_copy(
            src_ref=picked.at[part], dst_ref=far_picked.at[b, part],
            send_sem=pick_send.at[b, part], recv_sem=pick_recv.at[b, part],
            device_id=(partners[b],), device_id_type=MESH,
        )

    def send_tiles(g, piece, arriving=False):
        start = (my_place // 2**g) * 2**g
        if arriving:
            start = start + (1 - 2 * lax.rem(my_place // 2**g, 2)) * 2**g
        count = 2**g // pieces[g]
        group = tiles.at[pl.ds(start + piece * count, count)]
        return pltpu.make_async_remote_copy(
            src_ref=group, dst_ref=group,
            send_sem=tile_send.at[g, piece], recv_sem=tile_recv.at[g, piece],
            device_id=(partners[last - g],), device_id_type=MESH,
        )

    def wait_tiles(g):
        for piece in range(pieces[g]):
            send_tiles(g, piece, arriving=True).wait_recv()

    tile_load = pltpu.make_async_copy(tile_hbm, tiles.at[pl.ds(my_place, 1)], tile_sem)

    def start_load(c, carry):
        load_vox(c).start()
        return carry

    lax.fori_loop(0, chunks, start_load, 0)
    tile_load.start()
    for s in range(sections):
        load_weight(s).start()

    barrier = pltpu.get_barrier_semaphore()
    for b in range(sections):
        pl.semaphore_signal(barrier, inc=1, device_id=(partners[b],), device_id_type=MESH)
    pl.semaphore_wait(barrier, sections)

    def send_first(c, carry):
        load_vox(c).wait()
        send_section(0, c, 1).start()
        return carry

    lax.fori_loop(0, chunks, send_first, 0)
    offset = jnp.clip(pairs[1, me] - me * blocks, 0, blocks - 1)
    for part in range(parts):
        picked[part] = acts[0, offset * parts + part]
    tile_load.wait()
    send_tiles(0, 0).start()
    for b in (last, last - 1):
        for part in range(parts):
            send_picked(b, part).start()

    pick_step = {(b, part): 2 + b + 2 * part for b in range(last - 1) for part in range(parts)}
    tile_order = [(g, piece) for g in range(1, sections) for piece in range(pieces[g])]

    def mix(s, c):
        both = jnp.concatenate([acts[s, c], recv[s, c]], axis=1)
        place = pl.ds(pl.multiple_of((c // parts) * width, width), width)
        factors = jnp.concatenate([weights[s, 0, place, :], weights[s, 1, place, :]], axis=0)
        total = jnp.dot(both, factors, preferred_element_type=jnp.float32)
        return total.astype(jnp.bfloat16)

    def finish_chunk(c, carry):
        total = acts[sections, c].astype(jnp.float32)
        for b in range(sections):
            slot = pairs[0, partners[b]] - me * blocks
            mask = jnp.where(slot == c // parts, jnp.float32(1), jnp.float32(0))
            total = total + mask * terms[b, lax.rem(c, parts)]
        window(out, c)[...] = total.astype(jnp.bfloat16)
        return carry

    def make_term(index, carry):
        b, part = index // parts, lax.rem(index, parts)
        tile = tiles[carry[0]]
        for other in range(1, sections):
            tile = jnp.where(b == other, tiles[carry[other]], tile)
        terms[b, part] = jnp.dot(far_picked[b, part], tile, preferred_element_type=jnp.float32)
        return carry

    def step(t, carry):
        def section(s, stride):
            c = t - s - jnp.where(s == last, 1, 0)

            @pl.when(c == 0)
            def _():
                load_weight(s).wait()

            @pl.when((c >= 0) & (c < chunks))
            def _():
                send_section(s, c, stride).wait_recv()
                acts[s + 1, c] = mix(s, c)

                @pl.when(s < last)
                def _():
                    send_section(s + 1, c, 2 * stride).start()

            return 2 * stride

        lax.fori_loop(0, sections, section, 1)

        @pl.when(t == extra_step)
        def _():
            wait_tiles(last)
            for b in range(sections):
                for part in range(parts):
                    send_picked(b, part).wait_recv()
            wanted = tuple(reverse(owner[partners[b]]) for b in range(sections))
            lax.fori_loop(0, sections * parts, make_term, wanted)

        done = t - sections
        begin = jnp.where(t == extra_step, 0, done)
        stop = jnp.where(t >= extra_step, jnp.minimum(done + 1, chunks), begin)
        lax.fori_loop(begin, stop, finish_chunk, 0)

        for (b, part), when in pick_step.items():

            @pl.when(t == when)
            def _():
                send_picked(b, part).start()

        for when, (g, piece) in enumerate(tile_order):

            @pl.when(t == when + 1)
            def _():
                if piece == 0:
                    wait_tiles(g - 1)
                send_tiles(g, piece).start()

        return carry

    lax.fori_loop(0, max(chunks + sections, extra_step + 1), step, 0)

    for b in range(sections):
        for part in range(parts):
            send_picked(b, part).wait_send()
        for piece in range(pieces[b]):
            send_tiles(b, piece).wait_send()

    def drain(c, carry):
        def one(s, stride):
            send_section(s, c, stride).wait_send()
            return 2 * stride

        lax.fori_loop(0, sections, one, 1)
        return carry

    lax.fori_loop(0, chunks, drain, 0)


def per_device(voxel_rows, factor_weight, extra_weight, extra_pairs, tile_owner):
    devices = lax.axis_size("cols")
    sections = devices.bit_length() - 1
    batch, columns = voxel_rows.shape
    width = extra_weight.shape[1]
    blocks = columns // width
    parts = ROW_PARTS
    rows = batch // parts
    chunks = blocks * parts
    half = jnp.bfloat16
    dma = pltpu.SemaphoreType.DMA
    in_hbm = pl.BlockSpec(memory_space=pltpu.HBM)
    scalars = pl.BlockSpec(memory_space=pltpu.SMEM)
    return pl.pallas_call(
        functools.partial(butterfly_kernel, sections, blocks, parts),
        out_shape=pltpu.VMEM(voxel_rows.shape, half),
        in_specs=[in_hbm, in_hbm, in_hbm, scalars, scalars],
        out_specs=pl.BlockSpec(memory_space=pltpu.VMEM),
        scratch_shapes=[
            pltpu.VMEM((sections + 1, chunks, rows, width), half),
            pltpu.VMEM(factor_weight.shape, half),
            pltpu.VMEM((sections, chunks, rows, width), half),
            pltpu.VMEM((parts, rows, width), half),
            pltpu.VMEM((sections, parts, rows, width), half),
            pltpu.VMEM((devices, width, width), half),
            pltpu.VMEM((sections, parts, rows, width), jnp.float32),
            dma((chunks,)),
            dma((sections,)),
            dma,
            dma((sections, chunks)),
            dma((sections, chunks)),
            dma((sections, parts)),
            dma((sections, parts)),
            dma((sections, 4)),
            dma((sections, 4)),
        ],
        compiler_params=pltpu.CompilerParams(
            collective_id=0, has_side_effects=True, vmem_limit_bytes=VMEM_LIMIT
        ),
        cost_estimate=pl.CostEstimate(
            flops=4 * sections * batch * columns * width,
            bytes_accessed=4 * batch * columns + 4 * sections * columns * width,
            transcendentals=0,
        ),
        name="butterfly",
    )(voxel_rows, factor_weight, extra_weight, extra_pairs.T, tile_owner)


def solution(mesh):
    placed = (P(None, "cols"), P(None, None, "cols", None), P("cols", None, None), P(), P())
    return jax.shard_map(
        per_device, mesh=mesh, in_specs=placed, out_specs=P(None, "cols"), check_vma=False
    )
```

```python
import functools

import jax
import jax.numpy as jnp
from jax import lax
from jax.experimental import pallas as pl
from jax.experimental.pallas import tpu as pltpu
from jax.sharding import PartitionSpec as P

MESH = pl.DeviceIdType.MESH
ROW_PARTS = 2
FIRST_LEAD = 2
VMEM_LIMIT = 58 * 1024 * 1024


def butterfly_kernel(
    sections, blocks, parts,
    vox_hbm, factor_hbm, tile_hbm, pairs, owner, out,
    vox, weights, recv, hidden, picked, far_picked, tiles, terms,
    vox_sem, weight_sem, tile_sem,
    send_sem, recv_sem, pick_send, pick_recv, tile_send, tile_recv,
):
    me = lax.axis_index("cols")
    chunks, rows, width = vox.shape
    bits = [lax.rem(me // 2**b, 2) for b in range(sections)]
    partners = [me + (1 - 2 * bits[b]) * 2**b for b in range(sections)]
    last = sections - 1
    pieces = [min(2 ** max(g - 1, 0), 4) for g in range(sections)]
    lag = list(range(last)) + [last + 1]
    extra_step = sum(pieces) + 1

    def reverse(number):
        return sum(lax.rem(number // 2**b, 2) * 2 ** (last - b) for b in range(sections))

    my_place = reverse(me)

    def window(ref, c):
        row = pl.multiple_of(lax.rem(c, parts) * rows, rows)
        col = pl.multiple_of((c // parts) * width, width)
        return ref.at[pl.ds(row, rows), pl.ds(col, width)]

    def load_vox(c):
        return pltpu.make_async_copy(window(vox_hbm, c), vox.at[c], vox_sem.at[c])

    def load_weight(s):
        return pltpu.make_async_copy(factor_hbm.at[s], weights.at[s], weight_sem.at[s])

    def send_section(s, c):
        source = vox.at[c] if s == 0 else hidden.at[s - 1, c]
        return pltpu.make_async_remote_copy(
            src_ref=source, dst_ref=recv.at[s, c],
            send_sem=send_sem.at[s, c], recv_sem=recv_sem.at[s, c],
            device_id=(partners[s],), device_id_type=MESH,
        )

    def send_picked(b, part):
        return pltpu.make_async_remote_copy(
            src_ref=picked.at[part], dst_ref=far_picked.at[b, part],
            send_sem=pick_send.at[b, part], recv_sem=pick_recv.at[b, part],
            device_id=(partners[b],), device_id_type=MESH,
        )

    def send_tiles(g, piece, arriving=False):
        start = (my_place // 2**g) * 2**g
        if arriving:
            start = start + (1 - 2 * lax.rem(my_place // 2**g, 2)) * 2**g
        count = 2**g // pieces[g]
        group = tiles.at[pl.ds(start + piece * count, count)]
        return pltpu.make_async_remote_copy(
            src_ref=group, dst_ref=group,
            send_sem=tile_send.at[g, piece], recv_sem=tile_recv.at[g, piece],
            device_id=(partners[last - g],), device_id_type=MESH,
        )

    def wait_tiles(g):
        for piece in range(pieces[g]):
            send_tiles(g, piece, arriving=True).wait_recv()

    tile_load = pltpu.make_async_copy(tile_hbm, tiles.at[pl.ds(my_place, 1)], tile_sem)
    for c in range(chunks):
        load_vox(c).start()
    tile_load.start()
    for s in range(sections):
        load_weight(s).start()

    barrier = pltpu.get_barrier_semaphore()
    for b in range(sections):
        pl.semaphore_signal(barrier, inc=1, device_id=(partners[b],), device_id_type=MESH)
    pl.semaphore_wait(barrier, sections)

    for c in range(chunks):
        load_vox(c).wait()
    for c in range(min(FIRST_LEAD, chunks)):
        send_section(0, c).start()
    offset = jnp.clip(pairs[1, me] - me * blocks, 0, blocks - 1)
    for part in range(parts):
        picked[part] = vox[offset * parts + part]
    tile_load.wait()
    send_tiles(0, 0).start()
    for b in (last, last - 1):
        for part in range(parts):
            send_picked(b, part).start()

    pick_step = {(b, part): 2 + b + 2 * part for b in range(last - 1) for part in range(parts)}
    tile_order = [(g, piece) for g in range(1, sections) for piece in range(pieces[g])]

    def compute(s, c):
        i = c // parts
        if s == 0:
            own = vox[c]
        else:
            own = hidden[s - 1, c]
        both = jnp.concatenate([own, recv[s, c]], axis=1)
        place = pl.ds(pl.multiple_of(i * width, width), width)
        factors = jnp.concatenate([weights[s, 0, place, :], weights[s, 1, place, :]], axis=0)
        return jnp.dot(both, factors, preferred_element_type=jnp.float32)

    def add_extras(total, c):
        for b in range(sections):
            slot = pairs[0, partners[b]] - me * blocks
            mask = jnp.where(slot == c // parts, jnp.float32(1), jnp.float32(0))
            total = total + mask * terms[b, lax.rem(c, parts)]
        return total

    def finish_chunk(c, carry):
        place = window(out, c)
        place[...] = add_extras(place[...].astype(jnp.float32), c).astype(jnp.bfloat16)
        return carry

    def step(t, carry):
        @pl.when(t + FIRST_LEAD < chunks)
        def _():
            send_section(0, t + FIRST_LEAD).start()

        for s in range(sections):
            c = t - lag[s]

            @pl.when(c == 0)
            def _():
                load_weight(s).wait()

            @pl.when((c >= 0) & (c < chunks))
            def _():
                send_section(s, c).wait_recv()
                total = compute(s, c).astype(jnp.bfloat16)
                if s < last:
                    hidden[s, c] = total
                    send_section(s + 1, c).start()
                else:
                    window(out, c)[...] = total

        @pl.when(t == extra_step)
        def _():
            wait_tiles(last)
            for b in range(sections):
                for part in range(parts):
                    send_picked(b, part).wait_recv()
                tile = tiles[reverse(owner[partners[b]])]
                for part in range(parts):
                    terms[b, part] = jnp.dot(
                        far_picked[b, part], tile, preferred_element_type=jnp.float32
                    )
            lax.fori_loop(0, min(max(extra_step - lag[last], 0), chunks), finish_chunk, 0)

        c = t - lag[last]

        @pl.when((t >= extra_step) & (c >= 0) & (c < chunks))
        def _():
            finish_chunk(c, 0)

        for (b, part), when in pick_step.items():

            @pl.when(t == when)
            def _():
                send_picked(b, part).start()

        for when, (g, piece) in enumerate(tile_order):

            @pl.when(t == when + 1)
            def _():
                if piece == 0:
                    wait_tiles(g - 1)
                send_tiles(g, piece).start()

        return carry

    lax.fori_loop(0, max(chunks + lag[last], extra_step + 1), step, 0)

    for b in range(sections):
        for part in range(parts):
            send_picked(b, part).wait_send()
        for piece in range(pieces[b]):
            send_tiles(b, piece).wait_send()

    def finish(c, carry):
        for s in range(sections):
            send_section(s, c).wait_send()
        return carry

    lax.fori_loop(0, chunks, finish, 0)


def per_device(voxel_rows, factor_weight, extra_weight, extra_pairs, tile_owner):
    devices = lax.axis_size("cols")
    sections = devices.bit_length() - 1
    batch, columns = voxel_rows.shape
    width = extra_weight.shape[1]
    blocks = columns // width
    parts = ROW_PARTS
    rows = batch // parts
    chunks = blocks * parts
    half = jnp.bfloat16
    dma = pltpu.SemaphoreType.DMA
    in_hbm = pl.BlockSpec(memory_space=pltpu.HBM)
    scalars = pl.BlockSpec(memory_space=pltpu.SMEM)
    return pl.pallas_call(
        functools.partial(butterfly_kernel, sections, blocks, parts),
        out_shape=pltpu.VMEM(voxel_rows.shape, half),
        in_specs=[in_hbm, in_hbm, in_hbm, scalars, scalars],
        out_specs=pl.BlockSpec(memory_space=pltpu.VMEM),
        scratch_shapes=[
            pltpu.VMEM((chunks, rows, width), half),
            pltpu.VMEM(factor_weight.shape, half),
            pltpu.VMEM((sections, chunks, rows, width), half),
            pltpu.VMEM((sections - 1, chunks, rows, width), half),
            pltpu.VMEM((parts, rows, width), half),
            pltpu.VMEM((sections, parts, rows, width), half),
            pltpu.VMEM((devices, width, width), half),
            pltpu.VMEM((sections, parts, rows, width), jnp.float32),
            dma((chunks,)),
            dma((sections,)),
            dma,
            dma((sections, chunks)),
            dma((sections, chunks)),
            dma((sections, parts)),
            dma((sections, parts)),
            dma((sections, 4)),
            dma((sections, 4)),
        ],
        compiler_params=pltpu.CompilerParams(
            collective_id=0, has_side_effects=True, vmem_limit_bytes=VMEM_LIMIT
        ),
        cost_estimate=pl.CostEstimate(
            flops=4 * sections * batch * columns * width,
            bytes_accessed=4 * batch * columns + 4 * sections * columns * width,
            transcendentals=0,
        ),
        name="butterfly",
    )(voxel_rows, factor_weight, extra_weight, extra_pairs.T, tile_owner)


def solution(mesh):
    placed = (P(None, "cols"), P(None, None, "cols", None), P("cols", None, None), P(), P())
    return jax.shard_map(
        per_device, mesh=mesh, in_specs=placed, out_specs=P(None, "cols"), check_vma=False
    )
```

```python
import functools

import jax
import jax.numpy as jnp
from jax import lax
from jax.experimental import pallas as pl
from jax.experimental.pallas import tpu as pltpu
from jax.sharding import PartitionSpec as P

MESH = pl.DeviceIdType.MESH
ROW_PARTS = 3
FIRST_LEAD = 2
VMEM_LIMIT = 58 * 1024 * 1024


def butterfly_kernel(
    sections, blocks, parts,
    vox_hbm, factor_hbm, tile_hbm, pairs, owner, out,
    vox, weights, recv, hidden, picked, far_picked, tiles, terms,
    vox_sem, weight_sem, tile_sem,
    send_sem, recv_sem, pick_send, pick_recv, tile_send, tile_recv,
):
    me = lax.axis_index("cols")
    chunks, rows, width = vox.shape
    bits = [lax.rem(me // 2**b, 2) for b in range(sections)]
    partners = [me + (1 - 2 * bits[b]) * 2**b for b in range(sections)]
    last = sections - 1
    pieces = [min(2 ** max(g - 1, 0), 4) for g in range(sections)]
    lag = list(range(last - 1)) + [last, last + 2]
    extra_step = sum(pieces) + 1

    def reverse(number):
        return sum(lax.rem(number // 2**b, 2) * 2 ** (last - b) for b in range(sections))

    my_place = reverse(me)

    def window(ref, c):
        row = pl.multiple_of(lax.rem(c, parts) * rows, rows)
        col = pl.multiple_of((c // parts) * width, width)
        return ref.at[pl.ds(row, rows), pl.ds(col, width)]

    def load_vox(c):
        return pltpu.make_async_copy(window(vox_hbm, c), vox.at[c], vox_sem.at[c])

    def load_weight(s):
        return pltpu.make_async_copy(factor_hbm.at[s], weights.at[s], weight_sem.at[s])

    def send_section(s, c):
        source = vox.at[c] if s == 0 else hidden.at[s - 1, c]
        return pltpu.make_async_remote_copy(
            src_ref=source, dst_ref=recv.at[s, c],
            send_sem=send_sem.at[s, c], recv_sem=recv_sem.at[s, c],
            device_id=(partners[s],), device_id_type=MESH,
        )

    def send_picked(b, part):
        return pltpu.make_async_remote_copy(
            src_ref=picked.at[part], dst_ref=far_picked.at[b, part],
            send_sem=pick_send.at[b, part], recv_sem=pick_recv.at[b, part],
            device_id=(partners[b],), device_id_type=MESH,
        )

    def send_tiles(g, piece, arriving=False):
        start = (my_place // 2**g) * 2**g
        if arriving:
            start = start + (1 - 2 * lax.rem(my_place // 2**g, 2)) * 2**g
        count = 2**g // pieces[g]
        group = tiles.at[pl.ds(start + piece * count, count)]
        return pltpu.make_async_remote_copy(
            src_ref=group, dst_ref=group,
            send_sem=tile_send.at[g, piece], recv_sem=tile_recv.at[g, piece],
            device_id=(partners[last - g],), device_id_type=MESH,
        )

    def wait_tiles(g):
        for piece in range(pieces[g]):
            send_tiles(g, piece, arriving=True).wait_recv()

    tile_load = pltpu.make_async_copy(tile_hbm, tiles.at[pl.ds(my_place, 1)], tile_sem)
    for c in range(chunks):
        load_vox(c).start()
    tile_load.start()
    for s in range(sections):
        load_weight(s).start()

    barrier = pltpu.get_barrier_semaphore()
    for b in range(sections):
        pl.semaphore_signal(barrier, inc=1, device_id=(partners[b],), device_id_type=MESH)
    pl.semaphore_wait(barrier, sections)

    for c in range(chunks):
        load_vox(c).wait()
    for c in range(min(FIRST_LEAD, chunks)):
        send_section(0, c).start()
    offset = jnp.clip(pairs[1, me] - me * blocks, 0, blocks - 1)
    for part in range(parts):
        picked[part] = vox[offset * parts + part]
    tile_load.wait()
    send_tiles(0, 0).start()
    for b in (last, last - 1):
        for part in range(parts):
            send_picked(b, part).start()

    pick_step = {(b, part): 2 + b + 2 * part for b in range(last - 1) for part in range(parts)}
    tile_order = [(g, piece) for g in range(1, sections) for piece in range(pieces[g])]

    def compute(s, c):
        i = c // parts
        if s == 0:
            own = vox[c]
        else:
            own = hidden[s - 1, c]
        both = jnp.concatenate([own, recv[s, c]], axis=1)
        place = pl.ds(pl.multiple_of(i * width, width), width)
        factors = jnp.concatenate([weights[s, 0, place, :], weights[s, 1, place, :]], axis=0)
        return jnp.dot(both, factors, preferred_element_type=jnp.float32)

    def add_extras(total, c):
        for b in range(sections):
            slot = pairs[0, partners[b]] - me * blocks
            mask = jnp.where(slot == c // parts, jnp.float32(1), jnp.float32(0))
            total = total + mask * terms[b, lax.rem(c, parts)]
        return total

    def finish_chunk(c, carry):
        place = window(out, c)
        place[...] = add_extras(place[...].astype(jnp.float32), c).astype(jnp.bfloat16)
        return carry

    def step(t, carry):
        @pl.when(t + FIRST_LEAD < chunks)
        def _():
            send_section(0, t + FIRST_LEAD).start()

        for s in range(sections):
            c = t - lag[s]

            @pl.when(c == 0)
            def _():
                load_weight(s).wait()

            @pl.when((c >= 0) & (c < chunks))
            def _():
                send_section(s, c).wait_recv()
                total = compute(s, c).astype(jnp.bfloat16)
                if s < last:
                    hidden[s, c] = total
                    send_section(s + 1, c).start()
                else:
                    window(out, c)[...] = total

        @pl.when(t == extra_step)
        def _():
            wait_tiles(last)
            for b in range(sections):
                for part in range(parts):
                    send_picked(b, part).wait_recv()
                tile = tiles[reverse(owner[partners[b]])]
                for part in range(parts):
                    terms[b, part] = jnp.dot(
                        far_picked[b, part], tile, preferred_element_type=jnp.float32
                    )
            lax.fori_loop(0, min(max(extra_step - lag[last], 0), chunks), finish_chunk, 0)

        c = t - lag[last]

        @pl.when((t >= extra_step) & (c >= 0) & (c < chunks))
        def _():
            finish_chunk(c, 0)

        for (b, part), when in pick_step.items():

            @pl.when(t == when)
            def _():
                send_picked(b, part).start()

        for when, (g, piece) in enumerate(tile_order):

            @pl.when(t == when + 1)
            def _():
                if piece == 0:
                    wait_tiles(g - 1)
                send_tiles(g, piece).start()

        return carry

    lax.fori_loop(0, max(chunks + lag[last], extra_step + 1), step, 0)

    for b in range(sections):
        for part in range(parts):
            send_picked(b, part).wait_send()
        for piece in range(pieces[b]):
            send_tiles(b, piece).wait_send()

    def finish(c, carry):
        for s in range(sections):
            send_section(s, c).wait_send()
        return carry

    lax.fori_loop(0, chunks, finish, 0)


def per_device(voxel_rows, factor_weight, extra_weight, extra_pairs, tile_owner):
    devices = lax.axis_size("cols")
    sections = devices.bit_length() - 1
    batch, columns = voxel_rows.shape
    width = extra_weight.shape[1]
    blocks = columns // width
    parts = ROW_PARTS
    rows = batch // parts
    chunks = blocks * parts
    half = jnp.bfloat16
    dma = pltpu.SemaphoreType.DMA
    in_hbm = pl.BlockSpec(memory_space=pltpu.HBM)
    scalars = pl.BlockSpec(memory_space=pltpu.SMEM)
    return pl.pallas_call(
        functools.partial(butterfly_kernel, sections, blocks, parts),
        out_shape=pltpu.VMEM(voxel_rows.shape, half),
        in_specs=[in_hbm, in_hbm, in_hbm, scalars, scalars],
        out_specs=pl.BlockSpec(memory_space=pltpu.VMEM),
        scratch_shapes=[
            pltpu.VMEM((chunks, rows, width), half),
            pltpu.VMEM(factor_weight.shape, half),
            pltpu.VMEM((sections, chunks, rows, width), half),
            pltpu.VMEM((sections - 1, chunks, rows, width), half),
            pltpu.VMEM((parts, rows, width), half),
            pltpu.VMEM((sections, parts, rows, width), half),
            pltpu.VMEM((devices, width, width), half),
            pltpu.VMEM((sections, parts, rows, width), jnp.float32),
            dma((chunks,)),
            dma((sections,)),
            dma,
            dma((sections, chunks)),
            dma((sections, chunks)),
            dma((sections, parts)),
            dma((sections, parts)),
            dma((sections, 4)),
            dma((sections, 4)),
        ],
        compiler_params=pltpu.CompilerParams(
            collective_id=0, has_side_effects=True, vmem_limit_bytes=VMEM_LIMIT
        ),
        cost_estimate=pl.CostEstimate(
            flops=4 * sections * batch * columns * width,
            bytes_accessed=4 * batch * columns + 4 * sections * columns * width,
            transcendentals=0,
        ),
        name="butterfly",
    )(voxel_rows, factor_weight, extra_weight, extra_pairs.T, tile_owner)


def solution(mesh):
    placed = (P(None, "cols"), P(None, None, "cols", None), P("cols", None, None), P(), P())
    return jax.shard_map(
        per_device, mesh=mesh, in_specs=placed, out_specs=P(None, "cols"), check_vma=False
    )
```

```python
import functools

import jax
import jax.numpy as jnp
from jax import lax
from jax.experimental import pallas as pl
from jax.experimental.pallas import tpu as pltpu
from jax.sharding import PartitionSpec as P

MESH = pl.DeviceIdType.MESH
ROW_PARTS = 2
FIRST_LEAD = 2
VMEM_LIMIT = 58 * 1024 * 1024


def butterfly_kernel(
    sections, blocks, parts,
    vox_hbm, factor_hbm, tile_hbm, pairs, owner, out,
    vox, weights, recv, hidden, picked, far_picked, tiles, terms,
    vox_sem, weight_sem, tile_sem,
    send_sem, recv_sem, pick_send, pick_recv, tile_send, tile_recv,
):
    me = lax.axis_index("cols")
    chunks, rows, width = vox.shape
    bits = [lax.rem(me // 2**b, 2) for b in range(sections)]
    partners = [me + (1 - 2 * bits[b]) * 2**b for b in range(sections)]
    last = sections - 1
    pieces = [min(2 ** max(g - 1, 0), 4) for g in range(sections)]
    lag = list(range(sections))
    extra_step = sum(pieces) + 1

    def reverse(number):
        return sum(lax.rem(number // 2**b, 2) * 2 ** (last - b) for b in range(sections))

    my_place = reverse(me)

    def window(ref, c):
        row = pl.multiple_of(lax.rem(c, parts) * rows, rows)
        col = pl.multiple_of((c // parts) * width, width)
        return ref.at[pl.ds(row, rows), pl.ds(col, width)]

    def load_vox(c):
        return pltpu.make_async_copy(window(vox_hbm, c), vox.at[c], vox_sem.at[c])

    def load_weight(s):
        return pltpu.make_async_copy(factor_hbm.at[s], weights.at[s], weight_sem.at[s])

    def send_section(s, c):
        source = vox.at[c] if s == 0 else hidden.at[s - 1, c]
        return pltpu.make_async_remote_copy(
            src_ref=source, dst_ref=recv.at[s, c],
            send_sem=send_sem.at[s, c], recv_sem=recv_sem.at[s, c],
            device_id=(partners[s],), device_id_type=MESH,
        )

    def send_picked(b, part):
        return pltpu.make_async_remote_copy(
            src_ref=picked.at[part], dst_ref=far_picked.at[b, part],
            send_sem=pick_send.at[b, part], recv_sem=pick_recv.at[b, part],
            device_id=(partners[b],), device_id_type=MESH,
        )

    def send_tiles(g, piece, arriving=False):
        start = (my_place // 2**g) * 2**g
        if arriving:
            start = start + (1 - 2 * lax.rem(my_place // 2**g, 2)) * 2**g
        count = 2**g // pieces[g]
        group = tiles.at[pl.ds(start + piece * count, count)]
        return pltpu.make_async_remote_copy(
            src_ref=group, dst_ref=group,
            send_sem=tile_send.at[g, piece], recv_sem=tile_recv.at[g, piece],
            device_id=(partners[last - g],), device_id_type=MESH,
        )

    def wait_tiles(g):
        for piece in range(pieces[g]):
            send_tiles(g, piece, arriving=True).wait_recv()

    tile_load = pltpu.make_async_copy(tile_hbm, tiles.at[pl.ds(my_place, 1)], tile_sem)
    for c in range(chunks):
        load_vox(c).start()
    tile_load.start()
    for s in range(sections):
        load_weight(s).start()

    barrier = pltpu.get_barrier_semaphore()
    for b in range(sections):
        pl.semaphore_signal(barrier, inc=1, device_id=(partners[b],), device_id_type=MESH)
    pl.semaphore_wait(barrier, sections)

    for c in range(chunks):
        load_vox(c).wait()
    for c in range(min(FIRST_LEAD, chunks)):
        send_section(0, c).start()
    offset = jnp.clip(pairs[1, me] - me * blocks, 0, blocks - 1)
    for part in range(parts):
        picked[part] = vox[offset * parts + part]
    tile_load.wait()
    send_tiles(0, 0).start()
    for b in (last, last - 1):
        for part in range(parts):
            send_picked(b, part).start()

    pick_step = {(b, part): 2 + b + 2 * part for b in range(last - 1) for part in range(parts)}
    tile_order = [(g, piece) for g in range(1, sections) for piece in range(pieces[g])]

    def compute(s, c):
        i = c // parts
        if s == 0:
            own = vox[c]
        else:
            own = hidden[s - 1, c]
        both = jnp.concatenate([own, recv[s, c]], axis=1)
        place = pl.ds(pl.multiple_of(i * width, width), width)
        factors = jnp.concatenate([weights[s, 0, place, :], weights[s, 1, place, :]], axis=0)
        return jnp.dot(both, factors, preferred_element_type=jnp.float32)

    def add_extras(total, c):
        for b in range(sections):
            slot = pairs[0, partners[b]] - me * blocks
            mask = jnp.where(slot == c // parts, jnp.float32(1), jnp.float32(0))
            total = total + mask * terms[b, lax.rem(c, parts)]
        return total

    def finish_chunk(c, carry):
        place = window(out, c)
        place[...] = add_extras(place[...].astype(jnp.float32), c).astype(jnp.bfloat16)
        return carry

    def step(t, carry):
        @pl.when(t + FIRST_LEAD < chunks)
        def _():
            send_section(0, t + FIRST_LEAD).start()

        for s in range(sections):
            c = t - lag[s]

            @pl.when(c == 0)
            def _():
                load_weight(s).wait()

            @pl.when((c >= 0) & (c < chunks))
            def _():
                send_section(s, c).wait_recv()
                total = compute(s, c).astype(jnp.bfloat16)
                if s < last:
                    hidden[s, c] = total
                    send_section(s + 1, c).start()
                else:
                    window(out, c)[...] = total

        @pl.when(t == extra_step)
        def _():
            wait_tiles(last)
            for b in range(sections):
                for part in range(parts):
                    send_picked(b, part).wait_recv()
                tile = tiles[reverse(owner[partners[b]])]
                for part in range(parts):
                    terms[b, part] = jnp.dot(
                        far_picked[b, part], tile, preferred_element_type=jnp.float32
                    )
            lax.fori_loop(0, min(max(extra_step - lag[last], 0), chunks), finish_chunk, 0)

        c = t - lag[last]

        @pl.when((t >= extra_step) & (c >= 0) & (c < chunks))
        def _():
            finish_chunk(c, 0)

        for (b, part), when in pick_step.items():

            @pl.when(t == when)
            def _():
                send_picked(b, part).start()

        for when, (g, piece) in enumerate(tile_order):

            @pl.when(t == when + 1)
            def _():
                if piece == 0:
                    wait_tiles(g - 1)
                send_tiles(g, piece).start()

        return carry

    lax.fori_loop(0, max(chunks + lag[last], extra_step + 1), step, 0)

    for b in range(sections):
        for part in range(parts):
            send_picked(b, part).wait_send()
        for piece in range(pieces[b]):
            send_tiles(b, piece).wait_send()

    def finish(c, carry):
        for s in range(sections):
            send_section(s, c).wait_send()
        return carry

    lax.fori_loop(0, chunks, finish, 0)


def per_device(voxel_rows, factor_weight, extra_weight, extra_pairs, tile_owner):
    devices = lax.axis_size("cols")
    sections = devices.bit_length() - 1
    batch, columns = voxel_rows.shape
    width = extra_weight.shape[1]
    blocks = columns // width
    parts = ROW_PARTS
    rows = batch // parts
    chunks = blocks * parts
    half = jnp.bfloat16
    dma = pltpu.SemaphoreType.DMA
    in_hbm = pl.BlockSpec(memory_space=pltpu.HBM)
    scalars = pl.BlockSpec(memory_space=pltpu.SMEM)
    return pl.pallas_call(
        functools.partial(butterfly_kernel, sections, blocks, parts),
        out_shape=pltpu.VMEM(voxel_rows.shape, half),
        in_specs=[in_hbm, in_hbm, in_hbm, scalars, scalars],
        out_specs=pl.BlockSpec(memory_space=pltpu.VMEM),
        scratch_shapes=[
            pltpu.VMEM((chunks, rows, width), half),
            pltpu.VMEM(factor_weight.shape, half),
            pltpu.VMEM((sections, chunks, rows, width), half),
            pltpu.VMEM((sections - 1, chunks, rows, width), half),
            pltpu.VMEM((parts, rows, width), half),
            pltpu.VMEM((sections, parts, rows, width), half),
            pltpu.VMEM((devices, width, width), half),
            pltpu.VMEM((sections, parts, rows, width), jnp.float32),
            dma((chunks,)),
            dma((sections,)),
            dma,
            dma((sections, chunks)),
            dma((sections, chunks)),
            dma((sections, parts)),
            dma((sections, parts)),
            dma((sections, 4)),
            dma((sections, 4)),
        ],
        compiler_params=pltpu.CompilerParams(
            collective_id=0, has_side_effects=True, vmem_limit_bytes=VMEM_LIMIT
        ),
        cost_estimate=pl.CostEstimate(
            flops=4 * sections * batch * columns * width,
            bytes_accessed=4 * batch * columns + 4 * sections * columns * width,
            transcendentals=0,
        ),
        name="butterfly",
    )(voxel_rows, factor_weight, extra_weight, extra_pairs.T, tile_owner)


def solution(mesh):
    placed = (P(None, "cols"), P(None, None, "cols", None), P("cols", None, None), P(), P())
    return jax.shard_map(
        per_device, mesh=mesh, in_specs=placed, out_specs=P(None, "cols"), check_vma=False
    )
```
